32 devices in a mesh: parts: 2 (over x), tm: 16 (over z, y, core).
Axes of the slice: x: 2, y: 2, z: 4, core: 2. Of those that a mesh axis runs over, the one named last changes fastest.
Arguments:
- observations: float32 [256, 2048], P(('parts', 'tm')), parts along dimension 0, may hold values from -6 to 6
- outage_mask: int32 [256, 16], P(('parts', 'tm')), parts along dimension 0, may hold values 0 or 1
- group_length: int32 [32], P(('parts', 'tm')), parts along dimension 0, may hold values from 1 to 8, 96 in all
- prior_mean: float32 [4096], P('parts'), parts along dimension 0, may hold values from -8 to 8
- transition: float32 [16, 128, 128], replicated, may hold values from -1 to 1, as said below
- filter_gain: float32 [16, 128, 128], replicated, may hold values from -1 to 1, as said below
- smoother_gain: float32 [16, 128, 128], replicated, may hold values from -1 to 1, as said below
Outputs:
- smoothed: float32 [256, 2048], P(('parts', 'tm')), parts along dimension 0
The draws below stay inside these ranges and needn't reach their ends.
There are 2 independent parts, one for each index of `parts`. The reference program is written for one: setup_inputs(seed, part) draws one part's arguments, and reference() takes and returns one part's arrays. A program takes and returns all parts, laid end to end along the dimension named above; an argument that names none is the same for every part. Nothing has to cross between parts.
Inputs may be any that keep to these rules, and one draw needn't show every extreme that they name: `group_length`: live steps of each tm index; they sum to 96 and one entry equals 8. `transition`: nonzero only between states 2p and 2p + 1 of a block; spectral norm below 1. `filter_gain`: Symmetric, eigenvalues between 0 and 1. `smoother_gain`: spectral norm below 1.
All inputs are finite; a program needn't handle non-finite values. No bound on the sum of `outage_mask` or of `group_length` on one device may be relied on, other than what follows from the above.
Results may differ from the reference program's by a relative error of at most 0.0003.
Values sent between devices are 32-bit elements; how exact they have to be, the bound alone decides.
A program may use at most 320 MiB of HBM per device.

```python
import math
import jax
import jax.numpy as jnp
import numpy as np
from jax import lax

STATES = 2048
BLOCK = 128
CAP = 8
NBLK = 16
SLOTS = 128
N_TM = 16


def one_order(one_key):
    return jax.random.permutation(one_key, BLOCK // 2)


def pair_positions(key):
    keys = jax.random.split(jax.random.fold_in(key, 505), NBLK)
    orders = jax.vmap(one_order)(keys).astype(jnp.int32)
    inverse = jnp.argsort(orders, axis=1).astype(jnp.int32)
    within = jnp.arange(2, dtype=jnp.int32)
    return (2 * inverse[:, :, None] + within[None, None, :]).reshape(NBLK, BLOCK)


def mixed_rates(key, upper_rate, set_size):
    lower_rate = 0.2 / SLOTS
    span = jnp.log(jnp.float32(upper_rate / lower_rate))
    if set_size < BLOCK:
        level_draw = jax.random.uniform(jax.random.fold_in(key, 101), (NBLK, BLOCK // set_size), jnp.float32)
        factor = jax.random.uniform(jax.random.fold_in(key, 102), (NBLK, BLOCK), jnp.float32, 1.0, 2.0)
        levels = lower_rate * jnp.exp(level_draw * span)
        return jnp.repeat(levels, set_size, axis=1) * factor
    uniform_draw = jax.random.uniform(jax.random.fold_in(key, 101), (NBLK, BLOCK), jnp.float32)
    return lower_rate * jnp.exp(uniform_draw * span)


def section_angles(key, salt, section):
    return jax.random.uniform(jax.random.fold_in(key, salt + section), (NBLK, BLOCK), jnp.float32, 0.35, 1.2)


def turn_rows(matrix, angles, section):
    index_row = jnp.arange(BLOCK, dtype=jnp.int32)
    partner = jnp.bitwise_xor(index_row, 1 << section)
    lower = jnp.minimum(index_row, partner)
    chosen = angles[:, lower]
    signs = jnp.where(index_row < partner, -1.0, 1.0).astype(jnp.float32)
    cosine = jnp.cos(chosen)[:, :, None]
    sine_part = (signs[None, :] * jnp.sin(chosen))[:, :, None]
    return cosine * matrix + sine_part * matrix[:, partner, :]


def turn_columns(matrix, angles, section):
    index_row = jnp.arange(BLOCK, dtype=jnp.int32)
    partner = jnp.bitwise_xor(index_row, 1 << section)
    lower = jnp.minimum(index_row, partner)
    chosen = angles[:, lower]
    signs = jnp.where(index_row < partner, -1.0, 1.0).astype(jnp.float32)
    cosine = jnp.cos(chosen)[:, None, :]
    sine_part = (signs[None, :] * jnp.sin(chosen))[:, None, :]
    return cosine * matrix + sine_part * matrix[:, :, partner]


def reorder(matrix, positions):
    return matrix[positions][:, positions]


def spread(key, values, left_salt, right_salt, set_size):
    eye_mask = jnp.eye(BLOCK, dtype=jnp.float32) > 0.5
    matrix = jnp.where(eye_mask[None], values[:, :, None], jnp.float32(0.0))
    for section in range(set_size.bit_length() - 1):
        matrix = turn_rows(matrix, section_angles(key, left_salt, section), section)
        matrix = turn_columns(matrix, section_angles(key, right_salt, section), section)
    return jax.vmap(reorder)(matrix, pair_positions(key))


def draw_transition(key, part):
    upper_rate = 0.25
    set_size = BLOCK // 4
    rates_mixed = mixed_rates(key, upper_rate, set_size)
    rates_state = jnp.take_along_axis(rates_mixed, pair_positions(key), axis=1)
    angles = jax.random.uniform(jax.random.fold_in(key, 202), (NBLK, BLOCK // 2), jnp.float32, 0.3, 1.2)
    scales = 1.0 - rates_state[:, 0::2]
    cosine = scales * jnp.cos(angles)
    sine_part = scales * jnp.sin(angles)
    index_row = jnp.arange(BLOCK)
    pair_index = index_row // 2
    is_even = index_row % 2 == 0
    cos_rows = cosine[:, pair_index]
    sin_rows = sine_part[:, pair_index]
    same_pair = pair_index[:, None] == pair_index[None, :]
    diagonal_mask = index_row[:, None] == index_row[None, :]
    off_entries = jnp.where(is_even[None, :, None], -sin_rows[:, :, None], sin_rows[:, :, None])
    entries = jnp.where(diagonal_mask[None], cos_rows[:, :, None], off_entries)
    return jnp.where(same_pair[None], entries, jnp.float32(0.0))


def draw_filter_gain(key, part):
    upper_rate = 0.25
    set_size = BLOCK // 4
    rates_mixed = mixed_rates(key, upper_rate, set_size)
    matrix = spread(key, rates_mixed, 300, 300, set_size)
    return 0.5 * (matrix + jnp.swapaxes(matrix, 1, 2))


def draw_smoother_gain(key, part):
    upper_rate = 0.25
    set_size = BLOCK // 4
    rates_mixed = mixed_rates(key, upper_rate, set_size)
    return spread(key, 1.0 - rates_mixed, 400, 450, set_size)


def with_ends(drawn, stream_key, smallest, top_value):
    shape = drawn.shape
    place = [jax.random.randint(jax.random.fold_in(stream_key, axis), (), 0, shape[axis]) for axis in range(len(shape))]
    drawn = drawn.at[tuple(place)].set(smallest)
    longest = shape.index(max(shape))
    place[longest] = (place[longest] + 1) % shape[longest]
    return drawn.at[tuple(place)].set(top_value)


def block_levels(own_key, dims, cuts, least, top_value):
    def one(axis_at, blocks):
        steps = jax.random.uniform(jax.random.fold_in(jax.random.fold_in(own_key, 6), axis_at), (blocks,), jnp.float32, least / len(cuts), top_value / len(cuts))
        return jnp.repeat(jnp.exp(steps), dims[axis_at] // blocks).reshape((-1,) + (1,) * (len(dims) - axis_at - 1))

    level = one(*cuts[0])
    for cut in cuts[1:]:
        level = level * one(*cut)
    return level


def profile(number_of, total, bound, slope):
    loads = [(1 << 20) // math.isqrt(grade ** slope) + 1 for grade in range(2, number_of + 1)]
    surplus, counts = total - bound - (number_of - 1), [1] * (number_of - 1)
    while surplus > 0:
        candidates = [i for i in range(number_of - 1) if counts[i] < bound]
        whole, remaining = sum([loads[i] for i in candidates]), surplus
        for i in candidates:
            addition = min(bound - counts[i], max(1, remaining * loads[i] // whole), surplus)
            counts[i] = counts[i] + addition
            surplus = surplus - addition
    return np.array([bound] + counts)


def ragged(key, number_of, total, bound, skew):
    if number_of == 2:
        one = jax.random.randint(key, (), max(1, total - bound), min(bound, total - 1) + 1)
        return jnp.stack([one, total - one])
    sizes = jnp.asarray(profile(number_of, total, bound, skew), jnp.int32)
    pairs = (number_of - 1) // 2
    donor, sink = sizes[1:1 + 2 * pairs:2], sizes[2:2 + 2 * pairs:2]
    margin = jnp.minimum(donor - 1, bound - sink)
    moved = jax.random.randint(jax.random.fold_in(key, 1), (pairs,), 0, 1 << 20) % (margin + 1)
    sizes = sizes.at[1:1 + 2 * pairs:2].set(donor - moved).at[2:2 + 2 * pairs:2].set(sink + moved)
    return sizes[jax.random.permutation(jax.random.fold_in(key, 2), number_of)]


def noise(key, dims, scale, most, cuts=(), kind=jnp.bfloat16):
    values = jax.random.normal(key, dims, jnp.float32) * scale
    if len(cuts) > 0:
        values = block_levels(key, dims, cuts, -0.22, 0.18) * values
    return jnp.clip(values, min=-most, max=most).astype(kind)


def setup_inputs(seed: int = 0, part: int = 0) -> dict:
    seeds = jax.random.split(jax.random.key(seed), 8)
    part_keys = jax.random.split(jax.random.fold_in(seeds[7], part), 8)
    return {
        "observations": noise(part_keys[0], (SLOTS, STATES), 1.0, 6.0, ((0, 16),), jnp.float32),
        "outage_mask": with_ends((jax.random.randint(part_keys[1], (SLOTS, NBLK), 0, 4) < 3).astype(jnp.int32), jax.random.fold_in(part_keys[1], 1), 0, 1),
        "group_length": ragged(part_keys[2], N_TM, N_TM * CAP * 3 // 4, CAP, 1).astype(jnp.int32),
        "prior_mean": noise(part_keys[3], (STATES,), 2.0, 8.0, (), jnp.float32),
        "transition": draw_transition(jax.random.fold_in(seeds[7], 71), part),
        "filter_gain": draw_filter_gain(jax.random.fold_in(seeds[7], 71), part),
        "smoother_gain": draw_smoother_gain(jax.random.fold_in(seeds[7], 71), part),
    }


def reference(observations, outage_mask, group_length, prior_mean, transition, filter_gain, smoother_gain):
    highest = lax.Precision.HIGHEST
    identity_mat = jnp.eye(BLOCK, dtype=jnp.float32)
    updated = jnp.einsum('bij,bjk->bik', identity_mat - filter_gain, transition, precision=highest)
    back_keep = identity_mat - jnp.einsum('bij,bjk->bik', smoother_gain, transition, precision=highest)
    readings = observations.reshape(SLOTS, NBLK, BLOCK)
    position = jnp.arange(SLOTS, dtype=jnp.int32)
    alive_slot = (position % CAP) < group_length[position // CAP]
    observed = (outage_mask == 1) & alive_slot[:, None]
    gain_terms = jnp.einsum('bij,tbj->tbi', filter_gain, readings, precision=highest)

    def forward(state, inputs):
        is_seen, is_alive, gain_term = inputs
        step_mat = jnp.where(is_seen[:, None, None], updated, transition)
        moved_state = jnp.einsum('bij,bj->bi', step_mat, state, precision=highest)
        moved_state = moved_state + jnp.where(is_seen[:, None], gain_term, jnp.float32(0.0))
        moved_state = jnp.where(is_alive, moved_state, state)
        return moved_state, moved_state

    start_state = prior_mean.reshape(NBLK, BLOCK)
    _, filtered = lax.scan(forward, start_state, (observed, alive_slot, gain_terms))

    def backward(carried, inputs):
        later_state, started = carried
        state, is_alive = inputs
        recurred = jnp.einsum('bij,bj->bi', back_keep, state, precision=highest) + jnp.einsum('bij,bj->bi', smoother_gain, later_state, precision=highest)
        result = jnp.where(started, recurred, state)
        next_state = jnp.where(is_alive, result, later_state)
        return (next_state, started | is_alive), jnp.where(is_alive, result, jnp.float32(0.0))

    start_carry = (jnp.zeros((NBLK, BLOCK), jnp.float32), jnp.array(False))
    _, smoothed = lax.scan(backward, start_carry, (filtered, alive_slot), reverse=True)
    return smoothed.reshape(SLOTS, STATES)
```

```python
import functools

import jax
import jax.numpy as jnp
from jax import lax
from jax.experimental import pallas as pl
from jax.experimental.pallas import tpu as pltpu
from jax.sharding import PartitionSpec as P

highest = lax.Precision.HIGHEST
MESH = pl.DeviceIdType.MESH
WORD = 4


def mm(left, right):
    return jnp.dot(left, right, precision=highest, preferred_element_type=jnp.float32)


def radices_of(chunks):
    found, span = [], 1
    for radix in (4, 6, 4, 4, 4, 4):
        if span >= chunks:
            break
        found.append(radix)
        span *= radix
    return found


def iota(shape, axis):
    return lax.broadcasted_iota(jnp.int32, shape, axis)


def kernel(
    n,
    length_ref,
    mask_ref,
    obs_hbm,
    prior_ref,
    trans_hbm,
    filt_hbm,
    smooth_hbm,
    out_hbm,
    obs_v,
    stage,
    got,
    trans_v,
    filt_v,
    smooth_v,
    words,
    words_t,
    index_v,
    index_s,
    offsets,
    entries,
    buf_a,
    buf_b,
    result,
    load_sem,
    send_sem,
    recv_sem,
    send_sem2,
    recv_sem2,
    index_sem,
):
    cap = obs_v.shape[0]
    width = trans_v.shape[0]
    nblocks = trans_hbm.shape[0]
    share = n // nblocks
    slots = n * cap
    live = slots * 3 // 4
    chunks = live // WORD
    padded = -(-live // width) * width

    me = lax.axis_index("tm")
    block = me // share

    obs_load = pltpu.make_async_copy(obs_hbm, obs_v, load_sem.at[0])
    obs_load.start()
    loads = []
    for place, (source, target) in enumerate(
        ((trans_hbm, trans_v), (filt_hbm, filt_v), (smooth_hbm, smooth_v))
    ):
        load = pltpu.make_async_copy(source.at[block], target, load_sem.at[place + 1])
        load.start()
        loads.append(load)

    barrier = pltpu.get_barrier_semaphore()
    for step in range(1, n):
        pl.semaphore_signal(
            barrier, inc=1, device_id={"tm": lax.rem(me + step, n)}, device_id_type=MESH
        )

    length = length_ref[0]
    alive_here = (iota((cap, width), 0) < length).astype(jnp.float32)
    left_half = iota((cap, width), 1) < width // 2
    mask_f = mask_ref[...].astype(jnp.float32)
    for b in range(nblocks):
        seen = jnp.broadcast_to(mask_f[:, b : b + 1], (cap, width))
        stage[b, cap : 2 * cap, :] = jnp.where(left_half, seen * alive_here, alive_here)
    obs_load.wait()
    for b in range(nblocks):
        stage[b, 0:cap, :] = obs_v[:, b * width : (b + 1) * width]

    pl.semaphore_wait(barrier, n - 1)
    own_in = pltpu.make_async_copy(stage.at[block], got.at[me], recv_sem)
    own_in.start()
    for step in range(1, n):
        there = lax.rem(me + step, n)
        pltpu.make_async_remote_copy(
            src_ref=stage.at[there // share],
            dst_ref=got.at[me],
            send_sem=send_sem,
            recv_sem=recv_sem,
            device_id={"tm": there},
            device_id_type=MESH,
        ).start()

    for load in loads:
        load.wait()
    trans = trans_v[...]
    gain = filt_v[...]
    update = trans - mm(gain, trans)
    trans_t = trans.T
    update_t = update.T
    gain_t = gain.T
    smooth_t = smooth_v[...].T
    back_t = (iota((width, width), 0) == iota((width, width), 1)).astype(jnp.float32) - mm(
        trans_t, smooth_t
    )
    step_t = jnp.concatenate([update_t, trans_t], axis=1)
    square = mm(jnp.concatenate([trans, update], axis=0), jnp.concatenate([trans, update], axis=1))
    square_t = mm(
        jnp.concatenate([trans_t, update_t], axis=0), jnp.concatenate([trans_t, update_t], axis=1)
    )

    def tile(whole, row, column):
        return whole[row * width : (row + 1) * width, column * width : (column + 1) * width]

    pairs = [tile(square, hi, lo) for hi in range(2) for lo in range(2)]
    pairs_t = [tile(square_t, lo, hi) for hi in range(2) for lo in range(2)]
    pairs_row = jnp.concatenate(pairs, axis=1)
    pairs_t_row = jnp.concatenate(pairs_t, axis=1)
    for q in range(4):
        row = mm(pairs[q], pairs_row)
        row_t = mm(pairs_t[q], pairs_t_row)
        for p in range(4):
            words[4 * q + p] = row[:, p * width : (p + 1) * width]
            words_t[4 * p + q] = row_t[:, p * width : (p + 1) * width]

    radices = radices_of(chunks)
    levels = []
    base = smooth_t
    for radix in [WORD] + radices:
        powers = [base]
        while len(powers) < radix:
            have = len(powers)
            take = min(have, radix - have)
            more = mm(powers[-1], jnp.concatenate(powers[:take], axis=1) if take > 1 else powers[0])
            powers += [more[:, i * width : (i + 1) * width] for i in range(take)]
        levels.append(jnp.concatenate(powers[: radix - 1], axis=0))
        base = powers[radix - 1]

    pltpu.make_async_copy(got, got, recv_sem).wait()
    arrived = got[...]
    readings = arrived[:, 0:cap, :].reshape(slots, width)
    bits = arrived[:, cap : 2 * cap, :].reshape(slots, width)
    turned = pltpu.roll(bits, width // 2, 1)
    left = iota((slots, width), 1) < width // 2
    seen_slot = jnp.where(left, bits, turned)
    alive_slot = jnp.where(left, turned, bits)
    earlier = (iota((slots, slots), 1) < iota((slots, slots), 0)).astype(jnp.bfloat16)
    place = jnp.dot(
        earlier, alive_slot.astype(jnp.bfloat16), preferred_element_type=jnp.float32
    )
    pieces = []
    for first in range(0, padded, width):
        lane = iota((slots, width), 1) + first
        within = sum((lane >= s * chunks).astype(jnp.int32) for s in range(1, WORD))
        step_of = WORD * (lane - within * chunks) + within
        step_of = jnp.where(lane < live, step_of, -1)
        chosen = (alive_slot > 0.5) & (place.astype(jnp.int32) == step_of)
        pieces.append(chosen.astype(jnp.float32))
    spread = jnp.concatenate(pieces, axis=1) if len(pieces) > 1 else pieces[0]
    compact = mm(spread.T, jnp.concatenate([readings, seen_slot], axis=1))[:live]
    seen = [compact[s * chunks : (s + 1) * chunks, width:] > 0.5 for s in range(WORD)]
    index = sum(jnp.where(seen[s], 1 << s, 0) for s in range(WORD))
    index_v[...] = index
    index_copy = pltpu.make_async_copy(index_v, index_s, index_sem)
    index_copy.start()
    gained = mm(compact[:, :width], gain_t)
    gains = [
        jnp.where(seen[s], gained[s * chunks : (s + 1) * chunks], 0.0) for s in range(WORD)
    ]

    def advance(state, s):
        both = mm(state, step_t)
        return jnp.where(seen[s], both[:, :width], both[:, width:]) + gains[s]

    offset = gains[0]
    for s in range(1, WORD):
        offset = advance(offset, s)
    offsets[...] = offset
    index_copy.wait()

    eye = iota((width, width), 0) == iota((width, width), 1)
    group = 2
    entries[0:1, :] = prior_ref[:, pl.ds(pl.multiple_of(block * width, width), width)]

    def run(turn, state):
        for inner in range(group):
            c = turn * (2 * group) + 2 * inner
            terms = words[index_s[c, 0]] * state
            terms = terms + jnp.where(eye, offsets[pl.ds(c, 1), :], 0.0)
            column = jnp.sum(terms, axis=1, keepdims=True)
            entries[pl.ds(c + 1, 1), :] = jnp.sum(
                jnp.where(eye, column, 0.0), axis=0, keepdims=True
            )
            terms = words_t[index_s[c + 1, 0]] * column
            state = jnp.sum(terms, axis=0, keepdims=True) + offsets[pl.ds(c + 1, 1), :]
            entries[pl.ds(c + 2, 1), :] = state
        return state

    lax.fori_loop(0, chunks // (2 * group), run, entries[0:1, :])

    state = entries[0:chunks, :]
    filtered = []
    for s in range(WORD - 1):
        state = advance(state, s)
        filtered.append(state)
    filtered.append(entries[1 : chunks + 1, :])

    rows = jnp.concatenate(filtered, axis=0)
    recurred = mm(rows, back_t)
    is_end = iota((live, width), 0) == live - 1
    total = jnp.where(is_end, rows, recurred)

    tail = buf_a.shape[1] - chunks
    for s in range(WORD):
        buf_a[s, chunks:, :] = jnp.zeros((tail, width), jnp.float32)
        buf_b[s, chunks:, :] = jnp.zeros((tail, width), jnp.float32)
    stride = 1
    for level, radix in enumerate([WORD] + radices):
        buf = buf_a if level % 2 == 0 else buf_b
        for s in range(WORD):
            buf[s, 0:chunks, :] = total[s * chunks : (s + 1) * chunks]
        columns = []
        for i in range(1, radix):
            parts = []
            for s in range(WORD):
                ahead = s + i if level == 0 else s + i * stride
                parts.append(buf[ahead % WORD, pl.ds(ahead // WORD, chunks), :])
            columns.append(jnp.concatenate(parts, axis=0))
        total = total + mm(jnp.concatenate(columns, axis=1), levels[level])
        stride *= radix

    result[...] = mm(spread[:, :live], total).reshape(n, cap, width)

    column_of = pl.ds(pl.multiple_of(block * width, width), width)
    own_out = pltpu.make_async_copy(result.at[me], out_hbm.at[:, column_of], recv_sem2)
    own_out.start()
    for step in range(1, nblocks):
        there = lax.rem(me + step * share, n)
        pltpu.make_async_remote_copy(
            src_ref=result.at[there],
            dst_ref=out_hbm.at[:, column_of],
            send_sem=send_sem2,
            recv_sem=recv_sem2,
            device_id={"tm": there},
            device_id_type=MESH,
        ).start()
    sent = got.at[pl.ds(0, n - 1)]
    pltpu.make_async_copy(sent, sent, send_sem).wait()
    sent = result.at[pl.ds(0, nblocks - 1)]
    pltpu.make_async_copy(sent, sent, send_sem2).wait()
    pltpu.make_async_copy(out_hbm, out_hbm, recv_sem2).wait()


def shards(
    observations, outage_mask, group_length, prior_mean, transition, filter_gain, smoother_gain
):
    cap = observations.shape[0]
    nblocks, width, _ = transition.shape
    n = lax.axis_size("tm")
    chunks = n * cap * 3 // 4 // WORD
    reach = max([1] + [(r - 1) * s for r, s in zip(radices_of(chunks), strides_of(chunks))])
    tall = chunks + -(-reach // 8) * 8
    vmem, anywhere, smem = (
        pl.BlockSpec(memory_space=pltpu.VMEM),
        pl.BlockSpec(memory_space=pl.ANY),
        pl.BlockSpec(memory_space=pltpu.SMEM),
    )
    f32 = jnp.float32
    return pl.pallas_call(
        functools.partial(kernel, n),
        out_shape=jax.ShapeDtypeStruct(observations.shape, f32),
        in_specs=[smem, vmem, anywhere, vmem, anywhere, anywhere, anywhere],
        out_specs=anywhere,
        scratch_shapes=[
            pltpu.VMEM((cap, nblocks * width), f32),
            pltpu.VMEM((nblocks, 2 * cap, width), f32),
            pltpu.VMEM((n, 2 * cap, width), f32),
            pltpu.VMEM((width, width), f32),
            pltpu.VMEM((width, width), f32),
            pltpu.VMEM((width, width), f32),
            pltpu.VMEM((1 << WORD, width, width), f32),
            pltpu.VMEM((1 << WORD, width, width), f32),
            pltpu.VMEM((chunks, width), jnp.int32),
            pltpu.SMEM((chunks, width), jnp.int32),
            pltpu.VMEM((chunks, width), f32),
            pltpu.VMEM((chunks + 8, width), f32),
            pltpu.VMEM((WORD, tall, width), f32),
            pltpu.VMEM((WORD, tall, width), f32),
            pltpu.VMEM((n, cap, width), f32),
            pltpu.SemaphoreType.DMA((4,)),
            pltpu.SemaphoreType.DMA,
            pltpu.SemaphoreType.DMA,
            pltpu.SemaphoreType.DMA,
            pltpu.SemaphoreType.DMA,
            pltpu.SemaphoreType.DMA,
        ],
        compiler_params=pltpu.CompilerParams(
            collective_id=0, has_side_effects=True, vmem_limit_bytes=40 << 20
        ),
    )(
        group_length,
        outage_mask,
        observations,
        prior_mean.reshape(1, -1),
        transition,
        filter_gain,
        smoother_gain,
    )


def strides_of(chunks):
    strides, span = [], 1
    for radix in radices_of(chunks):
        strides.append(span)
        span *= radix
    return strides


def solution(mesh):
    placed = (
        P(("parts", "tm"), None),
        P(("parts", "tm"), None),
        P(("parts", "tm")),
        P("parts"),
        P(),
        P(),
        P(),
    )
    return jax.shard_map(
        shards, mesh=mesh, in_specs=placed, out_specs=P(("parts", "tm"), None), check_vma=False
    )
```

```python
import functools

import jax
import jax.numpy as jnp
from jax import lax
from jax.experimental import pallas as pl
from jax.experimental.pallas import tpu as pltpu
from jax.sharding import PartitionSpec as P

highest = lax.Precision.HIGHEST
MESH = pl.DeviceIdType.MESH
WORD = 3


def ready(weight):
    return weight


def mm(left, right):
    return jnp.dot(left, right, precision=highest, preferred_element_type=jnp.float32)


def choose(chosen, values):
    return jnp.dot(chosen, values, precision=highest, preferred_element_type=jnp.float32)


def radices_of(chunks):
    found, span = [], 1
    for radix in (6, 6, 4, 4, 4, 4):
        if span >= chunks:
            break
        found.append(radix)
        span *= radix
    return found


def iota(shape, axis):
    return lax.broadcasted_iota(jnp.int32, shape, axis)


def kernel(
    n,
    length_hbm,
    mask_hbm,
    obs_hbm,
    prior_hbm,
    trans_hbm,
    filt_hbm,
    smooth_hbm,
    out_hbm,
    length_s,
    mask_v,
    prior_v,
    obs_v,
    stage,
    got,
    trans_v,
    filt_v,
    smooth_v,
    words,
    words_t,
    index_v,
    index_s,
    offsets,
    entries,
    buf_a,
    buf_b,
    result,
    load_sem,
    send_sem,
    recv_sem,
    send_sem2,
    recv_sem2,
    index_sem,
):
    cap = obs_v.shape[0]
    width = trans_v.shape[0]
    half = width // 2
    nblocks = trans_hbm.shape[0]
    share = n // nblocks
    slots = n * cap
    live = slots * 3 // 4
    chunks = live // WORD
    padded = -(-live // width) * width

    me = lax.axis_index("tm")
    block = me // share

    loads = []
    for place, (source, target) in enumerate(
        (
            (length_hbm, length_s),
            (mask_hbm, mask_v),
            (obs_hbm, obs_v),
            (trans_hbm.at[block], trans_v),
            (filt_hbm.at[block], filt_v),
            (smooth_hbm.at[block], smooth_v),
            (prior_hbm, prior_v),
        )
    ):
        load = pltpu.make_async_copy(source, target, load_sem.at[place])
        load.start()
        loads.append(load)

    barrier = pltpu.get_barrier_semaphore()
    for step in range(1, n):
        pl.semaphore_signal(
            barrier, inc=1, device_id={"tm": lax.rem(me + step, n)}, device_id_type=MESH
        )

    loads[0].wait()
    loads[1].wait()
    length = length_s[0]
    alive_here = (iota((cap, width), 0) < length).astype(jnp.float32)
    lane = iota((cap, width), 1)
    left_half = lane < half
    own_slot = iota((cap, width), 0) * half + (lane - half) - me * cap
    alive_lanes = ((own_slot >= 0) & (own_slot < length)).astype(jnp.float32)
    mask_f = mask_v[...].astype(jnp.float32)
    for b in range(nblocks):
        seen = jnp.broadcast_to(mask_f[:, b : b + 1], (cap, width))
        stage[b, cap : 2 * cap, :] = jnp.where(left_half, seen * alive_here, alive_lanes)
    loads[2].wait()
    for b in range(nblocks):
        stage[b, 0:cap, :] = obs_v[:, b * width : (b + 1) * width]

    pl.semaphore_wait(barrier, n - 1)
    for step in range(1, n):
        there = lax.rem(me + step, n)
        pltpu.make_async_remote_copy(
            src_ref=stage.at[there // share],
            dst_ref=got.at[me],
            send_sem=send_sem,
            recv_sem=recv_sem,
            device_id={"tm": there},
            device_id_type=MESH,
        ).start()
    own_in = pltpu.make_async_copy(stage.at[block], got.at[me], recv_sem)
    own_in.start()

    for load in loads[3:]:
        load.wait()
    trans = trans_v[...]
    gain = filt_v[...]
    update = trans - mm(gain, ready(trans))
    trans_t = trans.T
    update_t = update.T
    gain_t = ready(gain.T)
    step_t = ready(jnp.concatenate([update_t, trans_t], axis=1))
    square = mm(
        jnp.concatenate([trans, update], axis=0),
        ready(jnp.concatenate([trans, update], axis=1)),
    )
    square_t = mm(
        jnp.concatenate([trans_t, update_t], axis=0),
        ready(jnp.concatenate([trans_t, update_t], axis=1)),
    )

    def tile(whole, row, column):
        return whole[row * width : (row + 1) * width, column * width : (column + 1) * width]

    pairs = [tile(square, hi, lo) for hi in range(2) for lo in range(2)]
    pairs_t = [tile(square_t, lo, hi) for hi in range(2) for lo in range(2)]
    cube = mm(
        jnp.concatenate([trans, update], axis=0), ready(jnp.concatenate(pairs, axis=1))
    )
    cube_t = mm(
        jnp.concatenate(pairs_t, axis=0),
        ready(jnp.concatenate([trans_t, update_t], axis=1)),
    )
    for last in range(2):
        for p in range(4):
            words[4 * last + p] = tile(cube, last, p)
            words_t[4 * last + p] = tile(cube_t, p, last)

    pltpu.make_async_copy(got, got, recv_sem).wait()
    arrived = got[...]
    readings = arrived[:, 0:cap, :].reshape(slots, width)
    bits = arrived[:, cap : 2 * cap, :].reshape(slots, width)
    seen_slot = jnp.where(iota((slots, width), 1) < half, bits, pltpu.roll(bits, half, 1))
    gained_slot = mm(readings, gain_t)
    alive_sum = jnp.sum(arrived[:, cap : 2 * cap, :], axis=0)
    alive_roll = pltpu.roll(alive_sum, half, 1)
    left_row = iota((1, width), 1) < half
    alive_row = jnp.concatenate(
        [
            jnp.where(left_row, alive_roll[2 * k : 2 * k + 1], alive_sum[2 * k + 1 : 2 * k + 2])
            for k in range(slots // width)
        ],
        axis=1,
    )
    earlier = (iota((slots, slots), 0) < iota((slots, slots), 1)).astype(jnp.bfloat16)
    place = jnp.dot(
        jnp.broadcast_to(alive_row, (16, slots)).astype(jnp.bfloat16),
        earlier,
        preferred_element_type=jnp.float32,
    )[0:1]
    place = jnp.where(alive_row > 0.5, place, -1.0)
    row = iota((padded, slots), 0)
    within = sum((row >= s * chunks).astype(jnp.int32) for s in range(1, WORD))
    step_of = WORD * (row - within * chunks) + within
    step_of = jnp.where(row < live, step_of, -2).astype(jnp.float32)
    gather = (jnp.broadcast_to(place, (padded, slots)) == step_of).astype(jnp.float32)
    compact = choose(gather, jnp.concatenate([gained_slot, seen_slot], axis=1))[:live]
    seen = [compact[s * chunks : (s + 1) * chunks, width:] > 0.5 for s in range(WORD)]
    index_v[...] = sum(jnp.where(seen[s], 1 << s, 0) for s in range(WORD))
    index_copy = pltpu.make_async_copy(index_v, index_s, index_sem)
    index_copy.start()
    gains = [
        jnp.where(seen[s], compact[s * chunks : (s + 1) * chunks, :width], 0.0)
        for s in range(WORD)
    ]

    def advance(state, s):
        both = mm(state, step_t)
        return jnp.where(seen[s], both[:, :width], both[:, width:]) + gains[s]

    offset = gains[0]
    for s in range(1, WORD):
        offset = advance(offset, s)
    offsets[...] = offset
    index_copy.wait()

    radices = [WORD] + radices_of(chunks)
    levels = []

    def powers_by_steps():
        base = smooth_v[...].T
        for level, radix in enumerate(radices):
            wanted = radix - 1 if level == len(radices) - 1 else radix
            powers = [base]
            while len(powers) < wanted:
                take = min(len(powers), wanted - len(powers))
                more = mm(powers[-1], ready(jnp.concatenate(powers[:take], axis=1)))
                powers += [more[:, i * width : (i + 1) * width] for i in range(take)]
                yield
            if level == 0:
                ends = mm(trans_t, ready(jnp.concatenate(powers, axis=1)))
                yield
                ends = [ends[:, i * width : (i + 1) * width] for i in range(radix)]
                eye_f = (iota((width, width), 0) == iota((width, width), 1)).astype(jnp.float32)
                starts = [l - e for l, e in zip([eye_f] + powers[: radix - 1], ends)]
                levels.append(ready(jnp.concatenate(starts, axis=0)))
                levels.append(ready(jnp.concatenate(ends, axis=1)))
            else:
                levels.append(ready(jnp.concatenate(powers[: radix - 1], axis=0)))
            base = powers[-1]

    side = powers_by_steps()

    eye = iota((width, width), 0) == iota((width, width), 1)
    state = prior_v[:, pl.ds(pl.multiple_of(block * width, width), width)]
    entries[0:1, :] = state
    for c in range(0, chunks, 2):
        terms = words[index_s[c, 0]] * state
        terms = terms + jnp.where(eye, offsets[c : c + 1, :], 0.0)
        column = jnp.sum(terms, axis=1, keepdims=True)
        entries[c + 1 : c + 2, :] = jnp.sum(jnp.where(eye, column, 0.0), axis=0, keepdims=True)
        terms = words_t[index_s[c + 1, 0]] * column
        state = jnp.sum(terms, axis=0, keepdims=True) + offsets[c + 1 : c + 2, :]
        entries[c + 2 : c + 3, :] = state
        next(side, None)
    for _ in side:
        pass

    state = entries[0:chunks, :]
    filtered = []
    for s in range(WORD - 1):
        state = advance(state, s)
        filtered.append(state)
    filtered.append(entries[1 : chunks + 1, :])
    newest = entries[chunks : chunks + 1, :]

    tail = buf_a.shape[1] - chunks
    for s in range(WORD):
        buf_a[s, chunks:, :] = jnp.zeros((tail, width), jnp.float32)
        buf_b[s, chunks:, :] = jnp.zeros((tail, width), jnp.float32)

    def ahead_of(buf, values, radix, stride):
        for s in range(WORD):
            buf[s, 0:chunks, :] = values[s]
        columns = []
        for i in range(1, radix):
            parts = []
            for s in range(WORD):
                later = s + i * stride
                parts.append(buf[later % WORD, later // WORD : later // WORD + chunks, :])
            columns.append(jnp.concatenate(parts, axis=0))
        return columns

    def by_step(rows):
        return [rows[s * chunks : (s + 1) * chunks] for s in range(WORD)]

    columns = [jnp.concatenate(filtered, axis=0)] + ahead_of(buf_a, filtered, WORD, 1)
    total = mm(jnp.concatenate(columns, axis=1), levels[0])
    finish = mm(jnp.broadcast_to(newest, (8, width)), levels[1])[0:1]
    is_end = iota((chunks, width), 0) == chunks - 1
    total = total + jnp.concatenate(
        [
            jnp.where(is_end, finish[:, i * width : (i + 1) * width], 0.0)
            for i in reversed(range(WORD))
        ],
        axis=0,
    )
    stride = WORD
    for level, radix in enumerate(radices[1:]):
        buf = buf_b if level % 2 == 0 else buf_a
        columns = ahead_of(buf, by_step(total), radix, stride)
        total = total + mm(jnp.concatenate(columns, axis=1), levels[level + 2])
        stride *= radix

    result[...] = choose(gather.T[:, :live], total).reshape(n, cap, width)

    column_of = pl.ds(pl.multiple_of(block * width, width), width)
    for step in range(1, nblocks):
        there = lax.rem(me + step * share, n)
        pltpu.make_async_remote_copy(
            src_ref=result.at[there],
            dst_ref=out_hbm.at[:, column_of],
            send_sem=send_sem2,
            recv_sem=recv_sem2,
            device_id={"tm": there},
            device_id_type=MESH,
        ).start()
    own_out = pltpu.make_async_copy(result.at[me], out_hbm.at[:, column_of], recv_sem2)
    own_out.start()
    sent = got.at[pl.ds(0, n - 1)]
    pltpu.make_async_copy(sent, sent, send_sem).wait()
    sent = result.at[pl.ds(0, nblocks - 1)]
    pltpu.make_async_copy(sent, sent, send_sem2).wait()
    pltpu.make_async_copy(out_hbm, out_hbm, recv_sem2).wait()


def shards(
    observations, outage_mask, group_length, prior_mean, transition, filter_gain, smoother_gain
):
    cap = observations.shape[0]
    nblocks, width, _ = transition.shape
    n = lax.axis_size("tm")
    chunks = n * cap * 3 // 4 // WORD
    reach = max([1] + [(r - 1) * s for r, s in zip(radices_of(chunks), strides_of(chunks))])
    tall = chunks + -(-reach // 8) * 8
    hbm = pl.BlockSpec(memory_space=pltpu.HBM)
    f32 = jnp.float32
    return pl.pallas_call(
        functools.partial(kernel, n),
        out_shape=jax.ShapeDtypeStruct(observations.shape, f32),
        in_specs=[hbm] * 7,
        out_specs=pl.BlockSpec(memory_space=pl.ANY),
        scratch_shapes=[
            pltpu.SMEM((1,), jnp.int32),
            pltpu.VMEM((cap, nblocks), jnp.int32),
            pltpu.VMEM((1, nblocks * width), f32),
            pltpu.VMEM((cap, nblocks * width), f32),
            pltpu.VMEM((nblocks, 2 * cap, width), f32),
            pltpu.VMEM((n, 2 * cap, width), f32),
            pltpu.VMEM((width, width), f32),
            pltpu.VMEM((width, width), f32),
            pltpu.VMEM((width, width), f32),
            pltpu.VMEM((1 << WORD, width, width), f32),
            pltpu.VMEM((1 << WORD, width, width), f32),
            pltpu.VMEM((chunks, width), jnp.int32),
            pltpu.SMEM((chunks, width), jnp.int32),
            pltpu.VMEM((chunks, width), f32),
            pltpu.VMEM((chunks + 8, width), f32),
            pltpu.VMEM((WORD, tall, width), f32),
            pltpu.VMEM((WORD, tall, width), f32),
            pltpu.VMEM((n, cap, width), f32),
            pltpu.SemaphoreType.DMA((7,)),
            pltpu.SemaphoreType.DMA,
            pltpu.SemaphoreType.DMA,
            pltpu.SemaphoreType.DMA,
            pltpu.SemaphoreType.DMA,
            pltpu.SemaphoreType.DMA,
        ],
        compiler_params=pltpu.CompilerParams(
            collective_id=0, has_side_effects=True, vmem_limit_bytes=64 << 20
        ),
    )(
        group_length,
        outage_mask,
        observations,
        prior_mean.reshape(1, -1),
        transition,
        filter_gain,
        smoother_gain,
    )


def strides_of(chunks):
    strides, span = [], 1
    for radix in radices_of(chunks):
        strides.append(span)
        span *= radix
    return strides


def solution(mesh):
    placed = (
        P(("parts", "tm"), None),
        P(("parts", "tm"), None),
        P(("parts", "tm")),
        P("parts"),
        P(),
        P(),
        P(),
    )
    return jax.shard_map(
        shards, mesh=mesh, in_specs=placed, out_specs=P(("parts", "tm"), None), check_vma=False
    )
```

```python
import functools

import jax
import jax.numpy as jnp
from jax import lax
from jax.experimental import pallas as pl
from jax.experimental.pallas import tpu as pltpu
from jax.sharding import PartitionSpec as P

MESH = pl.DeviceIdType.MESH
WORD = 3


def split(value):
    high = value.astype(jnp.bfloat16)
    return high, (value - high.astype(jnp.float32)).astype(jnp.bfloat16)


def ready(weight):
    high, low = split(weight)
    return jnp.concatenate([high, high, low], axis=0)


def mm(left, right):
    high, low = split(left)
    return jnp.dot(
        jnp.concatenate([high, low, high], axis=1), right, preferred_element_type=jnp.float32
    )


def choose(chosen, values):
    high, low = split(values)
    chosen = chosen.astype(jnp.bfloat16)
    return jnp.dot(
        jnp.concatenate([chosen, chosen], axis=1),
        jnp.concatenate([high, low], axis=0),
        preferred_element_type=jnp.float32,
    )


def radices_of(chunks):
    found, span = [], 1
    for radix in (6, 6, 4, 4, 4, 4):
        if span >= chunks:
            break
        found.append(radix)
        span *= radix
    return found


def iota(shape, axis):
    return lax.broadcasted_iota(jnp.int32, shape, axis)


def kernel(
    n,
    length_ref,
    mask_hbm,
    obs_hbm,
    prior_hbm,
    trans_hbm,
    filt_hbm,
    smooth_hbm,
    out_hbm,
    mask_v,
    prior_v,
    obs_v,
    stage,
    got,
    trans_v,
    filt_v,
    smooth_v,
    words,
    words_t,
    index_v,
    index_s,
    offsets,
    entries,
    buf_a,
    buf_b,
    result,
    load_sem,
    send_sem,
    recv_sem,
    send_sem2,
    recv_sem2,
    index_sem,
):
    cap = obs_v.shape[0]
    width = trans_v.shape[0]
    half = width // 2
    nblocks = trans_hbm.shape[0]
    share = n // nblocks
    slots = n * cap
    live = slots * 3 // 4
    chunks = live // WORD
    padded = -(-live // width) * width

    me = lax.axis_index("tm")
    block = me // share

    loads = []
    for place, (source, target) in enumerate(
        (
            (mask_hbm, mask_v),
            (obs_hbm, obs_v),
            (trans_hbm.at[block], trans_v),
            (filt_hbm.at[block], filt_v),
            (smooth_hbm.at[block], smooth_v),
            (prior_hbm, prior_v),
        )
    ):
        load = pltpu.make_async_copy(source, target, load_sem.at[place])
        load.start()
        loads.append(load)

    barrier = pltpu.get_barrier_semaphore()
    for step in range(1, n):
        pl.semaphore_signal(
            barrier, inc=1, device_id={"tm": lax.rem(me + step, n)}, device_id_type=MESH
        )

    loads[0].wait()
    length = length_ref[0]
    alive_here = (iota((cap, width), 0) < length).astype(jnp.float32)
    lane = iota((cap, width), 1)
    left_half = lane < half
    own_slot = iota((cap, width), 0) * half + (lane - half) - me * cap
    alive_lanes = ((own_slot >= 0) & (own_slot < length)).astype(jnp.float32)
    mask_f = mask_v[...].astype(jnp.float32)
    for b in range(nblocks):
        seen = jnp.broadcast_to(mask_f[:, b : b + 1], (cap, width))
        stage[b, cap : 2 * cap, :] = jnp.where(left_half, seen * alive_here, alive_lanes)
    loads[1].wait()
    for b in range(nblocks):
        stage[b, 0:cap, :] = obs_v[:, b * width : (b + 1) * width]

    pl.semaphore_wait(barrier, n - 1)
    for step in range(1, n):
        there = lax.rem(me + step, n)
        pltpu.make_async_remote_copy(
            src_ref=stage.at[there // share],
            dst_ref=got.at[me],
            send_sem=send_sem,
            recv_sem=recv_sem,
            device_id={"tm": there},
            device_id_type=MESH,
        ).start()
    own_in = pltpu.make_async_copy(stage.at[block], got.at[me], recv_sem)
    own_in.start()

    for load in loads[2:]:
        load.wait()
    trans = trans_v[...]
    gain = filt_v[...]
    update = trans - mm(gain, ready(trans))
    trans_t = trans.T
    update_t = update.T
    gain_t = ready(gain.T)
    step_t = ready(jnp.concatenate([update_t, trans_t], axis=1))
    square = mm(
        jnp.concatenate([trans, update], axis=0),
        ready(jnp.concatenate([trans, update], axis=1)),
    )
    square_t = mm(
        jnp.concatenate([trans_t, update_t], axis=0),
        ready(jnp.concatenate([trans_t, update_t], axis=1)),
    )

    def tile(whole, row, column):
        return whole[row * width : (row + 1) * width, column * width : (column + 1) * width]

    pairs = [tile(square, hi, lo) for hi in range(2) for lo in range(2)]
    pairs_t = [tile(square_t, lo, hi) for hi in range(2) for lo in range(2)]
    cube = mm(
        jnp.concatenate([trans, update], axis=0), ready(jnp.concatenate(pairs, axis=1))
    )
    cube_t = mm(
        jnp.concatenate(pairs_t, axis=0),
        ready(jnp.concatenate([trans_t, update_t], axis=1)),
    )
    for last in range(2):
        for p in range(4):
            words[4 * last + p] = tile(cube, last, p)
            words_t[4 * last + p] = tile(cube_t, p, last)

    pltpu.make_async_copy(got, got, recv_sem).wait()
    arrived = got[...]
    readings = arrived[:, 0:cap, :].reshape(slots, width)
    bits = arrived[:, cap : 2 * cap, :].reshape(slots, width)
    seen_slot = jnp.where(iota((slots, width), 1) < half, bits, pltpu.roll(bits, half, 1))
    gained_slot = mm(readings, gain_t)
    alive_sum = jnp.sum(arrived[:, cap : 2 * cap, :], axis=0)
    alive_roll = pltpu.roll(alive_sum, half, 1)
    left_row = iota((1, width), 1) < half
    alive_row = jnp.concatenate(
        [
            jnp.where(left_row, alive_roll[2 * k : 2 * k + 1], alive_sum[2 * k + 1 : 2 * k + 2])
            for k in range(slots // width)
        ],
        axis=1,
    )
    earlier = (iota((slots, slots), 0) < iota((slots, slots), 1)).astype(jnp.bfloat16)
    place = jnp.dot(
        jnp.broadcast_to(alive_row, (16, slots)).astype(jnp.bfloat16),
        earlier,
        preferred_element_type=jnp.float32,
    )[0:1]
    place = jnp.where(alive_row > 0.5, place, -1.0)
    row = iota((padded, slots), 0)
    within = sum((row >= s * chunks).astype(jnp.int32) for s in range(1, WORD))
    step_of = WORD * (row - within * chunks) + within
    step_of = jnp.where(row < live, step_of, -2).astype(jnp.float32)
    gather = (jnp.broadcast_to(place, (padded, slots)) == step_of).astype(jnp.float32)
    compact = choose(gather, jnp.concatenate([gained_slot, seen_slot], axis=1))[:live]
    seen = [compact[s * chunks : (s + 1) * chunks, width:] > 0.5 for s in range(WORD)]
    index_v[...] = sum(jnp.where(seen[s], 1 << s, 0) for s in range(WORD))
    index_copy = pltpu.make_async_copy(index_v, index_s, index_sem)
    index_copy.start()
    gains = [
        jnp.where(seen[s], compact[s * chunks : (s + 1) * chunks, :width], 0.0)
        for s in range(WORD)
    ]

    def advance(state, s):
        both = mm(state, step_t)
        return jnp.where(seen[s], both[:, :width], both[:, width:]) + gains[s]

    offset = gains[0]
    for s in range(1, WORD):
        offset = advance(offset, s)
    offsets[...] = offset
    index_copy.wait()

    radices = [WORD] + radices_of(chunks)
    levels = []

    def powers_by_steps():
        base = smooth_v[...].T
        for level, radix in enumerate(radices):
            wanted = radix - 1 if level == len(radices) - 1 else radix
            powers = [base]
            while len(powers) < wanted:
                take = min(len(powers), wanted - len(powers))
                more = mm(powers[-1], ready(jnp.concatenate(powers[:take], axis=1)))
                powers += [more[:, i * width : (i + 1) * width] for i in range(take)]
                yield
            if level == 0:
                ends = mm(trans_t, ready(jnp.concatenate(powers, axis=1)))
                yield
                ends = [ends[:, i * width : (i + 1) * width] for i in range(radix)]
                eye_f = (iota((width, width), 0) == iota((width, width), 1)).astype(jnp.float32)
                starts = [l - e for l, e in zip([eye_f] + powers[: radix - 1], ends)]
                levels.append(ready(jnp.concatenate(starts, axis=0)))
                levels.append(ready(jnp.concatenate(ends, axis=1)))
            else:
                levels.append(ready(jnp.concatenate(powers[: radix - 1], axis=0)))
            base = powers[-1]

    side = powers_by_steps()

    eye = iota((width, width), 0) == iota((width, width), 1)
    state = prior_v[:, pl.ds(pl.multiple_of(block * width, width), width)]
    entries[0:1, :] = state
    for c in range(0, chunks, 2):
        terms = words[index_s[c, 0]] * state
        terms = terms + jnp.where(eye, offsets[c : c + 1, :], 0.0)
        column = jnp.sum(terms, axis=1, keepdims=True)
        entries[c + 1 : c + 2, :] = jnp.sum(jnp.where(eye, column, 0.0), axis=0, keepdims=True)
        terms = words_t[index_s[c + 1, 0]] * column
        state = jnp.sum(terms, axis=0, keepdims=True) + offsets[c + 1 : c + 2, :]
        entries[c + 2 : c + 3, :] = state
        next(side, None)
    for _ in side:
        pass

    state = entries[0:chunks, :]
    filtered = []
    for s in range(WORD - 1):
        state = advance(state, s)
        filtered.append(state)
    filtered.append(entries[1 : chunks + 1, :])
    newest = entries[chunks : chunks + 1, :]

    tail = buf_a.shape[1] - chunks
    for s in range(WORD):
        buf_a[s, chunks:, :] = jnp.zeros((tail, width), jnp.float32)
        buf_b[s, chunks:, :] = jnp.zeros((tail, width), jnp.float32)

    def ahead_of(buf, values, radix, stride):
        for s in range(WORD):
            buf[s, 0:chunks, :] = values[s]
        columns = []
        for i in range(1, radix):
            parts = []
            for s in range(WORD):
                later = s + i * stride
                parts.append(buf[later % WORD, later // WORD : later // WORD + chunks, :])
            columns.append(jnp.concatenate(parts, axis=0))
        return columns

    def by_step(rows):
        return [rows[s * chunks : (s + 1) * chunks] for s in range(WORD)]

    columns = [jnp.concatenate(filtered, axis=0)] + ahead_of(buf_a, filtered, WORD, 1)
    total = mm(jnp.concatenate(columns, axis=1), levels[0])
    finish = mm(jnp.broadcast_to(newest, (16, width)), levels[1])[0:1]
    is_end = iota((chunks, width), 0) == chunks - 1
    total = total + jnp.concatenate(
        [
            jnp.where(is_end, finish[:, i * width : (i + 1) * width], 0.0)
            for i in reversed(range(WORD))
        ],
        axis=0,
    )
    stride = WORD
    for level, radix in enumerate(radices[1:]):
        buf = buf_b if level % 2 == 0 else buf_a
        columns = ahead_of(buf, by_step(total), radix, stride)
        total = total + mm(jnp.concatenate(columns, axis=1), levels[level + 2])
        stride *= radix

    result[...] = choose(gather.T[:, :live], total).reshape(n, cap, width)

    column_of = pl.ds(pl.multiple_of(block * width, width), width)
    for step in range(1, nblocks):
        there = lax.rem(me + step * share, n)
        pltpu.make_async_remote_copy(
            src_ref=result.at[there],
            dst_ref=out_hbm.at[:, column_of],
            send_sem=send_sem2,
            recv_sem=recv_sem2,
            device_id={"tm": there},
            device_id_type=MESH,
        ).start()
    own_out = pltpu.make_async_copy(result.at[me], out_hbm.at[:, column_of], recv_sem2)
    own_out.start()
    sent = got.at[pl.ds(0, n - 1)]
    pltpu.make_async_copy(sent, sent, send_sem).wait()
    sent = result.at[pl.ds(0, nblocks - 1)]
    pltpu.make_async_copy(sent, sent, send_sem2).wait()
    pltpu.make_async_copy(out_hbm, out_hbm, recv_sem2).wait()


def shards(
    observations, outage_mask, group_length, prior_mean, transition, filter_gain, smoother_gain
):
    cap = observations.shape[0]
    nblocks, width, _ = transition.shape
    n = lax.axis_size("tm")
    chunks = n * cap * 3 // 4 // WORD
    reach = max([1] + [(r - 1) * s for r, s in zip(radices_of(chunks), strides_of(chunks))])
    tall = chunks + -(-reach // 8) * 8
    hbm = pl.BlockSpec(memory_space=pltpu.HBM)
    f32 = jnp.float32
    return pl.pallas_call(
        functools.partial(kernel, n),
        out_shape=pltpu.VMEM(observations.shape, f32),
        in_specs=[pl.BlockSpec(memory_space=pltpu.SMEM)] + [hbm] * 6,
        out_specs=pl.BlockSpec(memory_space=pl.ANY),
        scratch_shapes=[
            pltpu.VMEM((cap, nblocks), jnp.int32),
            pltpu.VMEM((1, nblocks * width), f32),
            pltpu.VMEM((cap, nblocks * width), f32),
            pltpu.VMEM((nblocks, 2 * cap, width), f32),
            pltpu.VMEM((n, 2 * cap, width), f32),
            pltpu.VMEM((width, width), f32),
            pltpu.VMEM((width, width), f32),
            pltpu.VMEM((width, width), f32),
            pltpu.VMEM((1 << WORD, width, width), f32),
            pltpu.VMEM((1 << WORD, width, width), f32),
            pltpu.VMEM((chunks, width), jnp.int32),
            pltpu.SMEM((chunks, width), jnp.int32),
            pltpu.VMEM((chunks, width), f32),
            pltpu.VMEM((chunks + 8, width), f32),
            pltpu.VMEM((WORD, tall, width), f32),
            pltpu.VMEM((WORD, tall, width), f32),
            pltpu.VMEM((n, cap, width), f32),
            pltpu.SemaphoreType.DMA((6,)),
            pltpu.SemaphoreType.DMA,
            pltpu.SemaphoreType.DMA,
            pltpu.SemaphoreType.DMA,
            pltpu.SemaphoreType.DMA,
            pltpu.SemaphoreType.DMA,
        ],
        compiler_params=pltpu.CompilerParams(
            collective_id=0, has_side_effects=True, vmem_limit_bytes=48 << 20
        ),
    )(
        group_length,
        *(
            pltpu.with_memory_space_constraint(value, pltpu.HBM)
            for value in (
                outage_mask,
                observations,
                prior_mean.reshape(1, -1),
                transition,
                filter_gain,
                smoother_gain,
            )
        )
    )


def strides_of(chunks):
    strides, span = [], 1
    for radix in radices_of(chunks):
        strides.append(span)
        span *= radix
    return strides


def solution(mesh):
    placed = (
        P(("parts", "tm"), None),
        P(("parts", "tm"), None),
        P(("parts", "tm")),
        P("parts"),
        P(),
        P(),
        P(),
    )
    return jax.shard_map(
        shards, mesh=mesh, in_specs=placed, out_specs=P(("parts", "tm"), None), check_vma=False
    )
```

```python
import functools

import jax
import jax.numpy as jnp
from jax import lax
from jax.experimental import pallas as pl
from jax.experimental.pallas import tpu as pltpu
from jax.sharding import PartitionSpec as P

MESH = pl.DeviceIdType.MESH
WORD = 3
PER = 2


def split(value):
    high = value.astype(jnp.bfloat16)
    return high, (value - high.astype(jnp.float32)).astype(jnp.bfloat16)


def ready(weight):
    high, low = split(weight)
    return jnp.concatenate([high, high, low], axis=0)


def mm(left, right):
    high, low = split(left)
    return jnp.dot(
        jnp.concatenate([high, low, high], axis=1), right, preferred_element_type=jnp.float32
    )


def choose(chosen, values):
    high, low = split(values)
    chosen = chosen.astype(jnp.bfloat16)
    return jnp.dot(
        jnp.concatenate([chosen, chosen], axis=1),
        jnp.concatenate([high, low], axis=0),
        preferred_element_type=jnp.float32,
    )


def radices_of(chunks):
    found, span = [], 1
    for radix in (6, 6, 4, 4, 4, 4):
        if span >= chunks:
            break
        found.append(radix)
        span *= radix
    return found


def iota(shape, axis):
    return lax.broadcasted_iota(jnp.int32, shape, axis)


def kernel(
    n,
    length_ref,
    mask_hbm,
    obs_hbm,
    prior_hbm,
    trans_hbm,
    filt_hbm,
    smooth_hbm,
    out_hbm,
    alive_v,
    got_obs,
    got_mask,
    got_alive,
    prior_v,
    trans_v,
    filt_v,
    smooth_v,
    words,
    words_t,
    index_v,
    index_s,
    offsets,
    entries,
    buf_a,
    buf_b,
    result,
    load_sem,
    send_sem,
    recv_sem,
    out_sem,
    index_sem,
):
    cap, both = got_obs.shape[1:]
    width = trans_v.shape[1]
    nblocks = trans_hbm.shape[0]
    owners = nblocks // PER
    slots = n * cap
    live = slots * 3 // 4
    chunks = live // WORD
    padded = -(-live // width) * width

    me = lax.axis_index("tm")
    is_owner = me < owners
    block = me * PER
    mine = range(PER)

    def own_columns():
        return pl.ds(pl.multiple_of(me * both, both), both)

    loads = [
        pltpu.make_async_copy(source, target, load_sem.at[place])
        for place, (source, target) in enumerate(
            (
                (trans_hbm.at[pl.ds(block, PER)], trans_v),
                (filt_hbm.at[pl.ds(block, PER)], filt_v),
                (smooth_hbm.at[pl.ds(block, PER)], smooth_v),
                (prior_hbm, prior_v),
            )
        )
    ]

    barrier = pltpu.get_barrier_semaphore()

    def greet(there):
        pl.semaphore_signal(barrier, inc=1, device_id={"tm": there}, device_id_type=MESH)

    @pl.when(is_owner)
    def _():
        for load in loads:
            load.start()
        for step in range(1, n):
            greet(lax.rem(me + step, n))

    @pl.when(jnp.logical_not(is_owner))
    def _():
        for owner in range(owners):
            greet(owner)

    length = length_ref[0]
    own_slot = iota((cap, width), 0) * width + iota((cap, width), 1) - me * cap
    alive_v[...] = ((own_slot >= 0) & (own_slot < length)).astype(jnp.float32)

    @pl.when(is_owner)
    def _():
        pl.semaphore_wait(barrier, n - 1)

    @pl.when(jnp.logical_not(is_owner))
    def _():
        pl.semaphore_wait(barrier, owners)

    for owner in range(owners):
        parcels = (
            (alive_v, got_alive.at[me]),
            (mask_hbm, got_mask.at[me]),
            (obs_hbm.at[:, owner * both : (owner + 1) * both], got_obs.at[me]),
        )

        @pl.when(me != owner)
        def _():
            for kind, (source, target) in enumerate(parcels):
                pltpu.make_async_remote_copy(
                    src_ref=source,
                    dst_ref=target,
                    send_sem=send_sem.at[kind],
                    recv_sem=recv_sem.at[kind],
                    device_id={"tm": owner},
                    device_id_type=MESH,
                ).start()

        @pl.when(me == owner)
        def _():
            for kind, (source, target) in enumerate(parcels):
                pltpu.make_async_copy(source, target, recv_sem.at[kind]).start()

    @pl.when(is_owner)
    def _():
        for load in loads:
            load.wait()
        trans = [trans_v[j] for j in mine]
        gain = [filt_v[j] for j in mine]
        trans_t = [trans[j].T for j in mine]
        update = [trans[j] - mm(gain[j], ready(trans[j])) for j in mine]
        update_t = [update[j].T for j in mine]
        gain_t = [ready(gain[j].T) for j in mine]
        step_t = [ready(jnp.concatenate([update_t[j], trans_t[j]], axis=1)) for j in mine]

        def tile(whole, row, column):
            return whole[row * width : (row + 1) * width, column * width : (column + 1) * width]

        for j in mine:
            rows = jnp.concatenate([trans[j], update[j]], axis=0)
            square = mm(rows, ready(jnp.concatenate([trans[j], update[j]], axis=1)))
            square_t = mm(jnp.concatenate([trans_t[j], update_t[j]], axis=0), step_t[j])
            pairs = [tile(square, hi, lo) for hi in range(2) for lo in range(2)]
            pairs_t = [tile(square_t, lo, 1 - hi) for hi in range(2) for lo in range(2)]
            cube = mm(rows, ready(jnp.concatenate(pairs, axis=1)))
            cube_t = mm(jnp.concatenate(pairs_t, axis=0), step_t[j])
            for last in range(2):
                for p in range(4):
                    words[8 * j + 4 * last + p] = tile(cube, last, p)
                    words_t[8 * j + 4 * last + p] = tile(cube_t, p, 1 - last)

        for kind, got in enumerate((got_alive, got_mask, got_obs)):
            pltpu.make_async_copy(got, got, recv_sem.at[kind]).wait()
        readings = got_obs[...].reshape(slots, both)
        gained_slot = [
            mm(readings[:, j * width : (j + 1) * width], gain_t[j]) for j in mine
        ]
        alive_sum = jnp.sum(got_alive[...], axis=0)
        alive_row = jnp.concatenate(
            [alive_sum[k : k + 1] for k in range(slots // width)], axis=1
        )
        earlier = (iota((slots, slots), 0) < iota((slots, slots), 1)).astype(jnp.bfloat16)
        place = jnp.dot(
            jnp.broadcast_to(alive_row, (16, slots)).astype(jnp.bfloat16),
            earlier,
            preferred_element_type=jnp.float32,
        )[0:1]
        place = jnp.where(alive_row > 0.5, place, -1.0)
        mask = got_mask[...].reshape(slots, nblocks).astype(jnp.float32).astype(jnp.bfloat16)
        which = jnp.concatenate(
            [(iota((nblocks, width), 0) == block + j).astype(jnp.bfloat16) for j in mine], axis=1
        )
        seen_slot = jnp.dot(mask, which, preferred_element_type=jnp.float32)
        row = iota((padded, slots), 0)
        within = sum((row >= s * chunks).astype(jnp.int32) for s in range(1, WORD))
        step_of = WORD * (row - within * chunks) + within
        step_of = jnp.where(row < live, step_of, -2).astype(jnp.float32)
        gather = (jnp.broadcast_to(place, (padded, slots)) == step_of).astype(jnp.float32)
        seen_rows = jnp.dot(
            gather.astype(jnp.bfloat16),
            seen_slot.astype(jnp.bfloat16),
            preferred_element_type=jnp.float32,
        )

        def by_step(rows):
            return [rows[s * chunks : (s + 1) * chunks] for s in range(WORD)]

        seen = [
            [part > 0.5 for part in by_step(seen_rows[:, j * width : (j + 1) * width])]
            for j in mine
        ]
        for j in mine:
            index_v[j] = sum(jnp.where(seen[j][s], 1 << s, 0) for s in range(WORD))
        index_copy = pltpu.make_async_copy(index_v, index_s, index_sem)
        index_copy.start()
        gain_rows = choose(gather, jnp.concatenate(gained_slot, axis=1))
        gains = [
            [
                jnp.where(seen[j][s], part, 0.0)
                for s, part in enumerate(by_step(gain_rows[:, j * width : (j + 1) * width]))
            ]
            for j in mine
        ]

        def advance(j, state, s):
            moved = mm(state, step_t[j])
            return jnp.where(seen[j][s], moved[:, :width], moved[:, width:]) + gains[j][s]

        offset = [gains[j][0] for j in mine]
        for s in range(1, WORD):
            offset = [advance(j, offset[j], s) for j in mine]
        for j in mine:
            offsets[j] = offset[j]
        index_copy.wait()

        radices = [WORD] + radices_of(chunks)

        def powers_by_steps(j, levels):
            base = smooth_v[j].T
            for level, radix in enumerate(radices):
                wanted = radix - 1 if level == len(radices) - 1 else radix
                powers = [base]
                while len(powers) < wanted:
                    take = min(len(powers), wanted - len(powers))
                    more = mm(powers[-1], ready(jnp.concatenate(powers[:take], axis=1)))
                    powers += [more[:, i * width : (i + 1) * width] for i in range(take)]
                    yield
                if level == 0:
                    ends = mm(trans_t[j], ready(jnp.concatenate(powers, axis=1)))
                    yield
                    ends = [ends[:, i * width : (i + 1) * width] for i in range(radix)]
                    eye_f = (iota((width, width), 0) == iota((width, width), 1)).astype(
                        jnp.float32
                    )
                    starts = [l - e for l, e in zip([eye_f] + powers[: radix - 1], ends)]
                    levels.append(ready(jnp.concatenate(starts, axis=0)))
                    levels.append(ready(jnp.concatenate(ends, axis=1)))
                else:
                    levels.append(ready(jnp.concatenate(powers[: radix - 1], axis=0)))
                base = powers[-1]

        levels = [[] for j in mine]
        side = [powers_by_steps(j, levels[j]) for j in mine]

        eye = iota((width, width), 0) == iota((width, width), 1)
        state = [
            prior_v[:, pl.ds(pl.multiple_of((block + j) * width, width), width)] for j in mine
        ]
        for j in mine:
            entries[j, 0:1, :] = state[j]
        for c in range(0, chunks, 2):
            column = [None] * PER
            for j in mine:
                terms = words[8 * j + index_s[j, c, 0]] * state[j]
                terms = terms + jnp.where(eye, offsets[j, c : c + 1, :], 0.0)
                column[j] = jnp.sum(terms, axis=1, keepdims=True)
            for j in mine:
                entries[j, c + 1 : c + 2, :] = jnp.sum(
                    jnp.where(eye, column[j], 0.0), axis=0, keepdims=True
                )
                terms = words_t[8 * j + index_s[j, c + 1, 0]] * column[j]
                state[j] = jnp.sum(terms, axis=0, keepdims=True) + offsets[j, c + 1 : c + 2, :]
                entries[j, c + 2 : c + 3, :] = state[j]
                next(side[j], None)
        for j in mine:
            for _ in side[j]:
                pass

        state = [entries[j, 0:chunks, :] for j in mine]
        filtered = [[] for j in mine]
        for s in range(WORD - 1):
            for j in mine:
                state[j] = advance(j, state[j], s)
                filtered[j].append(state[j])
        for j in mine:
            filtered[j].append(entries[j, 1 : chunks + 1, :])

        tail = buf_a.shape[2] - chunks
        for j in mine:
            for s in range(WORD):
                buf_a[j, s, chunks:, :] = jnp.zeros((tail, width), jnp.float32)
                buf_b[j, s, chunks:, :] = jnp.zeros((tail, width), jnp.float32)

        def ahead_of(buf, j, values, radix, stride):
            for s in range(WORD):
                buf[j, s, 0:chunks, :] = values[s]
            columns = []
            for i in range(1, radix):
                parts = []
                for s in range(WORD):
                    later = s + i * stride
                    first = later // WORD
                    parts.append(buf[j, later % WORD, first : first + chunks, :])
                columns.append(jnp.concatenate(parts, axis=0))
            return columns

        total = [None] * PER
        for j in mine:
            columns = [jnp.concatenate(filtered[j], axis=0)]
            columns += ahead_of(buf_a, j, filtered[j], WORD, 1)
            total[j] = mm(jnp.concatenate(columns, axis=1), levels[j][0])
            newest = jnp.broadcast_to(entries[j, chunks : chunks + 1, :], (16, width))
            finish = mm(newest, levels[j][1])[0:1]
            is_end = iota((chunks, width), 0) == chunks - 1
            total[j] = total[j] + jnp.concatenate(
                [
                    jnp.where(is_end, finish[:, i * width : (i + 1) * width], 0.0)
                    for i in reversed(range(WORD))
                ],
                axis=0,
            )
        stride = WORD
        for level, radix in enumerate(radices[1:]):
            buf = buf_b if level % 2 == 0 else buf_a
            for j in mine:
                columns = ahead_of(buf, j, by_step(total[j]), radix, stride)
                total[j] = total[j] + mm(
                    jnp.concatenate(columns, axis=1), levels[j][level + 2]
                )
            stride *= radix

        spread = gather.T[:, :live]
        result[...] = choose(spread, jnp.concatenate(total, axis=1)).reshape(n, cap, both)

        for there in range(n):

            @pl.when(me != there)
            def _():
                pltpu.make_async_remote_copy(
                    src_ref=result.at[there],
                    dst_ref=out_hbm.at[:, own_columns()],
                    send_sem=send_sem.at[3],
                    recv_sem=out_sem,
                    device_id={"tm": there},
                    device_id_type=MESH,
                ).start()

            @pl.when(me == there)
            def _():
                pltpu.make_async_copy(
                    result.at[there], out_hbm.at[:, own_columns()], out_sem
                ).start()

        for kind, got in enumerate((got_alive, got_mask, got_obs)):
            sent = got.at[pl.ds(0, owners - 1)]
            pltpu.make_async_copy(sent, sent, send_sem.at[kind]).wait()
        sent = result.at[pl.ds(0, n - 1)]
        pltpu.make_async_copy(sent, sent, send_sem.at[3]).wait()

    @pl.when(jnp.logical_not(is_owner))
    def _():
        for kind, got in enumerate((got_alive, got_mask, got_obs)):
            sent = got.at[pl.ds(0, owners)]
            pltpu.make_async_copy(sent, sent, send_sem.at[kind]).wait()

    pltpu.make_async_copy(out_hbm, out_hbm, out_sem).wait()


def shards(
    observations, outage_mask, group_length, prior_mean, transition, filter_gain, smoother_gain
):
    cap = observations.shape[0]
    nblocks, width, _ = transition.shape
    n = lax.axis_size("tm")
    chunks = n * cap * 3 // 4 // WORD
    reach = max([1] + [(r - 1) * s for r, s in zip(radices_of(chunks), strides_of(chunks))])
    tall = chunks + -(-reach // 8) * 8
    hbm = pl.BlockSpec(memory_space=pltpu.HBM)
    f32 = jnp.float32
    return pl.pallas_call(
        functools.partial(kernel, n),
        out_shape=pltpu.VMEM(observations.shape, f32),
        in_specs=[pl.BlockSpec(memory_space=pltpu.SMEM)] + [hbm] * 6,
        out_specs=pl.BlockSpec(memory_space=pl.ANY),
        scratch_shapes=[
            pltpu.VMEM((cap, width), f32),
            pltpu.VMEM((n, cap, PER * width), f32),
            pltpu.VMEM((n, cap, nblocks), jnp.int32),
            pltpu.VMEM((n, cap, width), f32),
            pltpu.VMEM((1, nblocks * width), f32),
            pltpu.VMEM((PER, width, width), f32),
            pltpu.VMEM((PER, width, width), f32),
            pltpu.VMEM((PER, width, width), f32),
            pltpu.VMEM((PER << WORD, width, width), f32),
            pltpu.VMEM((PER << WORD, width, width), f32),
            pltpu.VMEM((PER, chunks, width), jnp.int32),
            pltpu.SMEM((PER, chunks, width), jnp.int32),
            pltpu.VMEM((PER, chunks, width), f32),
            pltpu.VMEM((PER, chunks + 8, width), f32),
            pltpu.VMEM((PER, WORD, tall, width), f32),
            pltpu.VMEM((PER, WORD, tall, width), f32),
            pltpu.VMEM((n, cap, PER * width), f32),
            pltpu.SemaphoreType.DMA((4,)),
            pltpu.SemaphoreType.DMA((4,)),
            pltpu.SemaphoreType.DMA((3,)),
            pltpu.SemaphoreType.DMA,
            pltpu.SemaphoreType.DMA,
        ],
        compiler_params=pltpu.CompilerParams(
            collective_id=0, has_side_effects=True, vmem_limit_bytes=48 << 20
        ),
    )(
        group_length,
        *(
            pltpu.with_memory_space_constraint(value, pltpu.HBM)
            for value in (
                outage_mask,
                observations,
                prior_mean.reshape(1, -1),
                transition,
                filter_gain,
                smoother_gain,
            )
        )
    )


def strides_of(chunks):
    strides, span = [], 1
    for radix in radices_of(chunks):
        strides.append(span)
        span *= radix
    return strides


def solution(mesh):
    placed = (
        P(("parts", "tm"), None),
        P(("parts", "tm"), None),
        P(("parts", "tm")),
        P("parts"),
        P(),
        P(),
        P(),
    )
    return jax.shard_map(
        shards, mesh=mesh, in_specs=placed, out_specs=P(("parts", "tm"), None), check_vma=False
    )
```

```python
import functools

import jax
import jax.numpy as jnp
from jax import lax
from jax.experimental import pallas as pl
from jax.experimental.pallas import tpu as pltpu
from jax.sharding import PartitionSpec as P

MESH = pl.DeviceIdType.MESH
WORD = 3
PER = 2


def split(value):
    high = value.astype(jnp.bfloat16)
    return high, (value - high.astype(jnp.float32)).astype(jnp.bfloat16)


def ready(weight):
    high, low = split(weight)
    return jnp.concatenate([high, high, low], axis=0)


def mm(left, right):
    high, low = split(left)
    return jnp.dot(
        jnp.concatenate([high, low, high], axis=1), right, preferred_element_type=jnp.float32
    )


def choose(chosen, values):
    high, low = split(values)
    chosen = chosen.astype(jnp.bfloat16)
    return jnp.dot(
        jnp.concatenate([chosen, chosen], axis=1),
        jnp.concatenate([high, low], axis=0),
        preferred_element_type=jnp.float32,
    )


def radices_of(chunks):
    found, span = [], 1
    for radix in (6, 6, 4, 4, 4, 4):
        if span >= chunks:
            break
        found.append(radix)
        span *= radix
    return found


def phases_of(n, cap, live, chunks):
    found = []
    for known in (n // 2, n - n // 4):
        sure = (live - (n - known) * cap) // WORD // 4 * 4
        found.append((known, sure))
    return found + [(n, chunks)]


def iota(shape, axis):
    return lax.broadcasted_iota(jnp.int32, shape, axis)


def kernel(
    n,
    length_ref,
    mask_hbm,
    obs_hbm,
    prior_hbm,
    trans_hbm,
    filt_hbm,
    smooth_hbm,
    out_hbm,
    alive_v,
    got_obs,
    got_mask,
    got_alive,
    prior_v,
    trans_v,
    filt_v,
    smooth_v,
    words,
    words_t,
    index_v,
    index_s,
    entries,
    buf_a,
    buf_b,
    result,
    load_sem,
    send_sem,
    recv_sem,
    out_sem,
    index_sem,
):
    cap, both = got_obs.shape[1:]
    width = trans_v.shape[1]
    nblocks = trans_hbm.shape[0]
    owners = nblocks // PER
    slots = n * cap
    live = slots * 3 // 4
    chunks = live // WORD
    padded = -(-live // width) * width

    me = lax.axis_index("tm")
    is_owner = me < owners
    block = me * PER
    mine = range(PER)

    def own_columns():
        return pl.ds(pl.multiple_of(me * both, both), both)

    loads = [
        pltpu.make_async_copy(source, target, load_sem.at[place])
        for place, (source, target) in enumerate(
            (
                (trans_hbm.at[pl.ds(block, PER)], trans_v),
                (filt_hbm.at[pl.ds(block, PER)], filt_v),
                (smooth_hbm.at[pl.ds(block, PER)], smooth_v),
                (prior_hbm, prior_v),
            )
        )
    ]

    barrier = pltpu.get_barrier_semaphore()

    def greet(there):
        pl.semaphore_signal(barrier, inc=1, device_id={"tm": there}, device_id_type=MESH)

    @pl.when(is_owner)
    def _():
        for load in loads:
            load.start()
        for step in range(1, n):
            greet(lax.rem(me + step, n))

    @pl.when(jnp.logical_not(is_owner))
    def _():
        for owner in range(owners):
            greet(owner)

    length = length_ref[0]
    own_slot = iota((cap, width), 0) * width + iota((cap, width), 1) - me * cap
    alive_v[...] = ((own_slot >= 0) & (own_slot < length)).astype(jnp.float32)

    @pl.when(is_owner)
    def _():
        pl.semaphore_wait(barrier, n - 1)

    @pl.when(jnp.logical_not(is_owner))
    def _():
        pl.semaphore_wait(barrier, owners)

    ends = [known for known, _ in phases_of(n, cap, live, chunks)]
    my_phase = sum((me >= known).astype(jnp.int32) for known in ends[:-1])
    for owner in range(owners):
        parcels = (
            (alive_v, got_alive.at[me]),
            (mask_hbm, got_mask.at[me]),
            (obs_hbm.at[:, owner * both : (owner + 1) * both], got_obs.at[me]),
        )

        @pl.when(me != owner)
        def _():
            for kind, (source, target) in enumerate(parcels):
                pltpu.make_async_remote_copy(
                    src_ref=source,
                    dst_ref=target,
                    send_sem=send_sem.at[kind],
                    recv_sem=recv_sem.at[3 * my_phase + kind],
                    device_id={"tm": owner},
                    device_id_type=MESH,
                ).start()

        @pl.when(me == owner)
        def _():
            for kind, (source, target) in enumerate(parcels):
                pltpu.make_async_copy(
                    source, target, recv_sem.at[3 * my_phase + kind]
                ).start()

    @pl.when(is_owner)
    def _():
        for load in loads:
            load.wait()
        trans = [trans_v[j] for j in mine]
        gain = [filt_v[j] for j in mine]
        trans_t = [trans[j].T for j in mine]
        update = [trans[j] - mm(gain[j], ready(trans[j])) for j in mine]
        update_t = [update[j].T for j in mine]
        gain_t = [ready(gain[j].T) for j in mine]
        step_t = [ready(jnp.concatenate([update_t[j], trans_t[j]], axis=1)) for j in mine]

        def tile(whole, row, column):
            return whole[row * width : (row + 1) * width, column * width : (column + 1) * width]

        for j in mine:
            rows = jnp.concatenate([trans[j], update[j]], axis=0)
            square = mm(rows, ready(jnp.concatenate([trans[j], update[j]], axis=1)))
            square_t = mm(jnp.concatenate([trans_t[j], update_t[j]], axis=0), step_t[j])
            pairs = [tile(square, hi, lo) for hi in range(2) for lo in range(2)]
            pairs_t = [tile(square_t, lo, 1 - hi) for hi in range(2) for lo in range(2)]
            cube = mm(rows, ready(jnp.concatenate(pairs, axis=1)))
            cube_t = mm(jnp.concatenate(pairs_t, axis=0), step_t[j])
            for last in range(2):
                for p in range(4):
                    words[8 * j + 4 * last + p] = tile(cube, last, p)
                    words_t[8 * j + 4 * last + p] = tile(cube_t, p, 1 - last)

        def by_step(rows, count):
            return [rows[s * count : (s + 1) * count] for s in range(WORD)]

        radices = [WORD] + radices_of(chunks)

        def powers_by_steps(j, levels):
            base = smooth_v[j].T
            for level, radix in enumerate(radices):
                wanted = radix - 1 if level == len(radices) - 1 else radix
                powers = [base]
                while len(powers) < wanted:
                    take = min(len(powers), wanted - len(powers))
                    more = mm(powers[-1], ready(jnp.concatenate(powers[:take], axis=1)))
                    powers += [more[:, i * width : (i + 1) * width] for i in range(take)]
                    yield
                if level == 0:
                    ends = mm(trans_t[j], ready(jnp.concatenate(powers, axis=1)))
                    yield
                    ends = [ends[:, i * width : (i + 1) * width] for i in range(radix)]
                    eye_f = (iota((width, width), 0) == iota((width, width), 1)).astype(
                        jnp.float32
                    )
                    starts = [l - e for l, e in zip([eye_f] + powers[: radix - 1], ends)]
                    levels.append(ready(jnp.concatenate(starts, axis=0)))
                    levels.append(ready(jnp.concatenate(ends, axis=1)))
                else:
                    levels.append(ready(jnp.concatenate(powers[: radix - 1], axis=0)))
                base = powers[-1]

        levels = [[] for j in mine]
        side = [powers_by_steps(j, levels[j]) for j in mine]
        eye = iota((width, width), 0) == iota((width, width), 1)
        state = [
            prior_v[:, pl.ds(pl.multiple_of((block + j) * width, width), width)] for j in mine
        ]
        for j in mine:
            entries[j, 0:1, :] = state[j]
        earlier = (iota((slots, slots), 0) < iota((slots, slots), 1)).astype(jnp.bfloat16)
        which = jnp.concatenate(
            [(iota((nblocks, width), 0) == block + j).astype(jnp.bfloat16) for j in mine], axis=1
        )
        alive_sum = jnp.zeros((cap, width), jnp.float32)
        gained_slot = [[] for j in mine]
        seen_slot = []
        filtered = [[[] for s in range(WORD)] for j in mine]

        first_device, first = 0, 0
        for phase, (known, until) in enumerate(phases_of(n, cap, live, chunks)):
            count = until - first
            for kind, got in enumerate((got_alive, got_mask, got_obs)):
                part = got.at[pl.ds(first_device, known - first_device)]
                pltpu.make_async_copy(part, part, recv_sem.at[3 * phase + kind]).wait()
            fresh = (known - first_device) * cap
            here = known * cap
            readings = got_obs[first_device:known].reshape(fresh, both)
            for j in mine:
                gained_slot[j].append(
                    mm(readings[:, j * width : (j + 1) * width], gain_t[j])
                )
            mask = got_mask[first_device:known].reshape(fresh, nblocks)
            mask = mask.astype(jnp.float32).astype(jnp.bfloat16)
            seen_slot.append(jnp.dot(mask, which, preferred_element_type=jnp.float32))
            alive_sum = alive_sum + jnp.sum(got_alive[first_device:known], axis=0)
            alive_row = jnp.concatenate(
                [alive_sum[k : k + 1] for k in range(slots // width)], axis=1
            )
            place = jnp.dot(
                jnp.broadcast_to(alive_row, (16, slots)).astype(jnp.bfloat16),
                earlier,
                preferred_element_type=jnp.float32,
            )[0:1]
            place = jnp.where(alive_row > 0.5, place, -1.0)
            rows = -(-WORD * count // 16) * 16
            row = iota((rows, slots), 0)
            within = sum((row >= s * count).astype(jnp.int32) for s in range(1, WORD))
            step_of = WORD * (first + row - within * count) + within
            step_of = jnp.where(row < WORD * count, step_of, -2).astype(jnp.float32)
            gather = (jnp.broadcast_to(place, (rows, slots)) == step_of).astype(jnp.float32)
            gather = gather[:, :here]
            seen_rows = jnp.dot(
                gather.astype(jnp.bfloat16),
                jnp.concatenate(seen_slot, axis=0).astype(jnp.bfloat16),
                preferred_element_type=jnp.float32,
            )
            seen = [
                [part > 0.5 for part in by_step(seen_rows[:, j * width : (j + 1) * width], count)]
                for j in mine
            ]
            index_v[phase] = jnp.zeros(index_v.shape[1:], jnp.int32)
            for j in mine:
                index_v[phase, j, 0:count, :] = sum(
                    jnp.where(seen[j][s], 1 << s, 0) for s in range(WORD)
                )
            index_copy = pltpu.make_async_copy(
                index_v.at[phase], index_s.at[phase], index_sem.at[phase]
            )
            index_copy.start()
            gain_rows = choose(
                gather,
                jnp.concatenate(
                    [jnp.concatenate(gained_slot[j], axis=0) for j in mine], axis=1
                ),
            )
            gains = [
                [
                    jnp.where(seen[j][s], part, 0.0)
                    for s, part in enumerate(
                        by_step(gain_rows[:, j * width : (j + 1) * width], count)
                    )
                ]
                for j in mine
            ]

            def advance(j, value, s):
                moved = mm(value, step_t[j])
                return jnp.where(seen[j][s], moved[:, :width], moved[:, width:]) + gains[j][s]

            offset = [gains[j][0] for j in mine]
            for s in range(1, WORD):
                offset = [advance(j, offset[j], s) for j in mine]
            index_copy.wait()

            for c in range(0, count, 2):
                column = [None] * PER
                for j in mine:
                    terms = words[8 * j + index_s[phase, j, c, 0]] * state[j]
                    terms = terms + jnp.where(eye, offset[j][c : c + 1, :], 0.0)
                    column[j] = jnp.sum(terms, axis=1, keepdims=True)
                for j in mine:
                    at = first + c + 1
                    entries[j, at : at + 1, :] = jnp.sum(
                        jnp.where(eye, column[j], 0.0), axis=0, keepdims=True
                    )
                    terms = words_t[8 * j + index_s[phase, j, c + 1, 0]] * column[j]
                    state[j] = jnp.sum(terms, axis=0, keepdims=True) + offset[j][c + 1 : c + 2, :]
                    entries[j, at + 1 : at + 2, :] = state[j]
                    next(side[j], None)

            inner = [entries[j, first:until, :] for j in mine]
            for s in range(WORD - 1):
                for j in mine:
                    inner[j] = advance(j, inner[j], s)
                    filtered[j][s].append(inner[j])
            for j in mine:
                filtered[j][WORD - 1].append(entries[j, first + 1 : until + 1, :])
            first_device, first = known, until
        for j in mine:
            for _ in side[j]:
                pass
        filtered = [[jnp.concatenate(parts, axis=0) for parts in filtered[j]] for j in mine]

        place = jnp.broadcast_to(place, (padded, slots))
        row = iota((padded, slots), 0)
        within = sum((row >= s * chunks).astype(jnp.int32) for s in range(1, WORD))
        step_of = WORD * (row - within * chunks) + within
        step_of = jnp.where(row < live, step_of, -2).astype(jnp.float32)
        spread = (place == step_of).astype(jnp.float32).T[:, :live]

        tail = buf_a.shape[2] - chunks
        for j in mine:
            for s in range(WORD):
                buf_a[j, s, chunks:, :] = jnp.zeros((tail, width), jnp.float32)
                buf_b[j, s, chunks:, :] = jnp.zeros((tail, width), jnp.float32)

        def ahead_of(buf, j, values, radix, stride):
            for s in range(WORD):
                buf[j, s, 0:chunks, :] = values[s]
            columns = []
            for i in range(1, radix):
                parts = []
                for s in range(WORD):
                    later = s + i * stride
                    first = later // WORD
                    parts.append(buf[j, later % WORD, first : first + chunks, :])
                columns.append(jnp.concatenate(parts, axis=0))
            return columns

        total = [None] * PER
        for j in mine:
            columns = [jnp.concatenate(filtered[j], axis=0)]
            columns += ahead_of(buf_a, j, filtered[j], WORD, 1)
            total[j] = mm(jnp.concatenate(columns, axis=1), levels[j][0])
            newest = jnp.broadcast_to(entries[j, chunks : chunks + 1, :], (16, width))
            finish = mm(newest, levels[j][1])[0:1]
            is_end = iota((chunks, width), 0) == chunks - 1
            total[j] = total[j] + jnp.concatenate(
                [
                    jnp.where(is_end, finish[:, i * width : (i + 1) * width], 0.0)
                    for i in reversed(range(WORD))
                ],
                axis=0,
            )
        stride = WORD
        for level, radix in enumerate(radices[1:]):
            buf = buf_b if level % 2 == 0 else buf_a
            for j in mine:
                columns = ahead_of(buf, j, by_step(total[j], chunks), radix, stride)
                total[j] = total[j] + mm(
                    jnp.concatenate(columns, axis=1), levels[j][level + 2]
                )
            stride *= radix

        result[...] = choose(spread, jnp.concatenate(total, axis=1)).reshape(n, cap, both)

        for there in range(n):

            @pl.when(me != there)
            def _():
                pltpu.make_async_remote_copy(
                    src_ref=result.at[there],
                    dst_ref=out_hbm.at[:, own_columns()],
                    send_sem=send_sem.at[3],
                    recv_sem=out_sem,
                    device_id={"tm": there},
                    device_id_type=MESH,
                ).start()

            @pl.when(me == there)
            def _():
                pltpu.make_async_copy(
                    result.at[there], out_hbm.at[:, own_columns()], out_sem
                ).start()

        for kind, got in enumerate((got_alive, got_mask, got_obs)):
            sent = got.at[pl.ds(0, owners - 1)]
            pltpu.make_async_copy(sent, sent, send_sem.at[kind]).wait()
        sent = result.at[pl.ds(0, n - 1)]
        pltpu.make_async_copy(sent, sent, send_sem.at[3]).wait()

    @pl.when(jnp.logical_not(is_owner))
    def _():
        for kind, got in enumerate((got_alive, got_mask, got_obs)):
            sent = got.at[pl.ds(0, owners)]
            pltpu.make_async_copy(sent, sent, send_sem.at[kind]).wait()

    pltpu.make_async_copy(out_hbm, out_hbm, out_sem).wait()


def shards(
    observations, outage_mask, group_length, prior_mean, transition, filter_gain, smoother_gain
):
    cap = observations.shape[0]
    nblocks, width, _ = transition.shape
    n = lax.axis_size("tm")
    chunks = n * cap * 3 // 4 // WORD
    reach = max([1] + [(r - 1) * s for r, s in zip(radices_of(chunks), strides_of(chunks))])
    tall = chunks + -(-reach // 8) * 8
    hbm = pl.BlockSpec(memory_space=pltpu.HBM)
    f32 = jnp.float32
    return pl.pallas_call(
        functools.partial(kernel, n),
        out_shape=pltpu.VMEM(observations.shape, f32),
        in_specs=[pl.BlockSpec(memory_space=pltpu.SMEM)] + [hbm] * 6,
        out_specs=pl.BlockSpec(memory_space=pl.ANY),
        scratch_shapes=[
            pltpu.VMEM((cap, width), f32),
            pltpu.VMEM((n, cap, PER * width), f32),
            pltpu.VMEM((n, cap, nblocks), jnp.int32),
            pltpu.VMEM((n, cap, width), f32),
            pltpu.VMEM((1, nblocks * width), f32),
            pltpu.VMEM((PER, width, width), f32),
            pltpu.VMEM((PER, width, width), f32),
            pltpu.VMEM((PER, width, width), f32),
            pltpu.VMEM((PER << WORD, width, width), f32),
            pltpu.VMEM((PER << WORD, width, width), f32),
            pltpu.VMEM((3, PER, chunks, width), jnp.int32),
            pltpu.SMEM((3, PER, chunks, width), jnp.int32),
            pltpu.VMEM((PER, chunks + 8, width), f32),
            pltpu.VMEM((PER, WORD, tall, width), f32),
            pltpu.VMEM((PER, WORD, tall, width), f32),
            pltpu.VMEM((n, cap, PER * width), f32),
            pltpu.SemaphoreType.DMA((4,)),
            pltpu.SemaphoreType.DMA((4,)),
            pltpu.SemaphoreType.DMA((9,)),
            pltpu.SemaphoreType.DMA,
            pltpu.SemaphoreType.DMA((3,)),
        ],
        compiler_params=pltpu.CompilerParams(
            collective_id=0, has_side_effects=True, vmem_limit_bytes=48 << 20
        ),
    )(
        group_length,
        *(
            pltpu.with_memory_space_constraint(value, pltpu.HBM)
            for value in (
                outage_mask,
                observations,
                prior_mean.reshape(1, -1),
                transition,
                filter_gain,
                smoother_gain,
            )
        )
    )


def strides_of(chunks):
    strides, span = [], 1
    for radix in radices_of(chunks):
        strides.append(span)
        span *= radix
    return strides


def solution(mesh):
    placed = (
        P(("parts", "tm"), None),
        P(("parts", "tm"), None),
        P(("parts", "tm")),
        P("parts"),
        P(),
        P(),
        P(),
    )
    return jax.shard_map(
        shards, mesh=mesh, in_specs=placed, out_specs=P(("parts", "tm"), None), check_vma=False
    )
```

```python
import functools

import jax
import jax.numpy as jnp
from jax import lax
from jax.experimental import pallas as pl
from jax.experimental.pallas import tpu as pltpu
from jax.sharding import PartitionSpec as P

MESH = pl.DeviceIdType.MESH
WORD = 3


def split(value):
    high = value.astype(jnp.bfloat16)
    return high, (value - high.astype(jnp.float32)).astype(jnp.bfloat16)


def ready(weight):
    high, low = split(weight)
    return jnp.concatenate([high, high, low], axis=0)


def mm(left, right):
    high, low = split(left)
    return jnp.dot(
        jnp.concatenate([high, low, high], axis=1), right, preferred_element_type=jnp.float32
    )


def choose(chosen, values):
    high, low = split(values)
    chosen = chosen.astype(jnp.bfloat16)
    return jnp.dot(
        jnp.concatenate([chosen, chosen], axis=1),
        jnp.concatenate([high, low], axis=0),
        preferred_element_type=jnp.float32,
    )


def radices_of(chunks):
    found, span = [], 1
    for radix in (6, 6, 4, 4, 4, 4):
        if span >= chunks:
            break
        found.append(radix)
        span *= radix
    return found


def iota(shape, axis):
    return lax.broadcasted_iota(jnp.int32, shape, axis)


def kernel(
    n,
    length_ref,
    mask_hbm,
    obs_hbm,
    prior_hbm,
    trans_hbm,
    filt_hbm,
    smooth_hbm,
    out_hbm,
    mask_v,
    prior_v,
    obs_v,
    stage,
    got,
    trans_v,
    filt_v,
    smooth_v,
    words,
    words_t,
    index_v,
    index_s,
    offsets,
    entries,
    buf_a,
    buf_b,
    result,
    load_sem,
    send_sem,
    recv_sem,
    send_sem2,
    recv_sem2,
    index_sem,
):
    cap = obs_v.shape[0]
    width = trans_v.shape[0]
    half = width // 2
    nblocks = trans_hbm.shape[0]
    share = n // nblocks
    slots = n * cap
    live = slots * 3 // 4
    chunks = live // WORD
    padded = -(-live // width) * width

    me = lax.axis_index("tm")
    block = me // share

    loads = []
    for place, (source, target) in enumerate(
        (
            (mask_hbm, mask_v),
            (obs_hbm, obs_v),
            (trans_hbm.at[block], trans_v),
            (filt_hbm.at[block], filt_v),
            (smooth_hbm.at[block], smooth_v),
            (prior_hbm, prior_v),
        )
    ):
        load = pltpu.make_async_copy(source, target, load_sem.at[place])
        load.start()
        loads.append(load)

    barrier = pltpu.get_barrier_semaphore()
    for step in range(1, n):
        pl.semaphore_signal(
            barrier, inc=1, device_id={"tm": lax.rem(me + step, n)}, device_id_type=MESH
        )

    loads[0].wait()
    length = length_ref[0]
    alive_here = (iota((cap, width), 0) < length).astype(jnp.float32)
    lane = iota((cap, width), 1)
    left_half = lane < half
    own_slot = iota((cap, width), 0) * half + (lane - half) - me * cap
    alive_lanes = ((own_slot >= 0) & (own_slot < length)).astype(jnp.float32)
    mask_f = mask_v[...].astype(jnp.float32)
    for b in range(nblocks):
        seen = jnp.broadcast_to(mask_f[:, b : b + 1], (cap, width))
        stage[b, cap : 2 * cap, :] = jnp.where(left_half, seen * alive_here, alive_lanes)
    loads[1].wait()
    for b in range(nblocks):
        stage[b, 0:cap, :] = obs_v[:, b * width : (b + 1) * width]

    pl.semaphore_wait(barrier, n - 1)
    for step in range(1, n):
        there = lax.rem(me + step, n)
        pltpu.make_async_remote_copy(
            src_ref=stage.at[there // share],
            dst_ref=got.at[me],
            send_sem=send_sem,
            recv_sem=recv_sem,
            device_id={"tm": there},
            device_id_type=MESH,
        ).start()
    own_in = pltpu.make_async_copy(stage.at[block], got.at[me], recv_sem)
    own_in.start()

    for load in loads[2:]:
        load.wait()
    trans = trans_v[...]
    gain = filt_v[...]
    update = trans - mm(gain, ready(trans))
    trans_t = trans.T
    update_t = update.T
    gain_t = ready(gain.T)
    square = mm(
        jnp.concatenate([trans, update], axis=0),
        ready(jnp.concatenate([trans, update], axis=1)),
    )
    square_t = mm(
        jnp.concatenate([trans_t, update_t], axis=0),
        ready(jnp.concatenate([trans_t, update_t], axis=1)),
    )

    def tile(whole, row, column):
        return whole[row * width : (row + 1) * width, column * width : (column + 1) * width]

    pairs = [tile(square, hi, lo) for hi in range(2) for lo in range(2)]
    pairs_t = [tile(square_t, lo, hi) for hi in range(2) for lo in range(2)]
    moves = ready(jnp.concatenate([update_t, trans_t] + pairs_t, axis=1))
    cube = mm(
        jnp.concatenate([trans, update], axis=0), ready(jnp.concatenate(pairs, axis=1))
    )
    cube_t = mm(
        jnp.concatenate(pairs_t, axis=0),
        ready(jnp.concatenate([trans_t, update_t], axis=1)),
    )
    for last in range(2):
        for p in range(4):
            words[4 * last + p] = tile(cube, last, p)
            words_t[4 * last + p] = tile(cube_t, p, last)

    pltpu.make_async_copy(got, got, recv_sem).wait()
    arrived = got[...]
    readings = arrived[:, 0:cap, :].reshape(slots, width)
    bits = arrived[:, cap : 2 * cap, :].reshape(slots, width)
    seen_slot = jnp.where(iota((slots, width), 1) < half, bits, pltpu.roll(bits, half, 1))
    gained_slot = mm(readings, gain_t)
    alive_sum = jnp.sum(arrived[:, cap : 2 * cap, :], axis=0)
    alive_roll = pltpu.roll(alive_sum, half, 1)
    left_row = iota((1, width), 1) < half
    alive_row = jnp.concatenate(
        [
            jnp.where(left_row, alive_roll[2 * k : 2 * k + 1], alive_sum[2 * k + 1 : 2 * k + 2])
            for k in range(slots // width)
        ],
        axis=1,
    )
    earlier = (iota((slots, slots), 0) < iota((slots, slots), 1)).astype(jnp.bfloat16)
    place = jnp.dot(
        jnp.broadcast_to(alive_row, (16, slots)).astype(jnp.bfloat16),
        earlier,
        preferred_element_type=jnp.float32,
    )[0:1]
    place = jnp.where(alive_row > 0.5, place, -1.0)
    row = iota((padded, slots), 0)
    within = sum((row >= s * chunks).astype(jnp.int32) for s in range(1, WORD))
    step_of = WORD * (row - within * chunks) + within
    step_of = jnp.where(row < live, step_of, -2).astype(jnp.float32)
    gather = (jnp.broadcast_to(place, (padded, slots)) == step_of).astype(jnp.float32)
    compact = choose(gather, jnp.concatenate([gained_slot, seen_slot], axis=1))[:live]
    seen = [compact[s * chunks : (s + 1) * chunks, width:] > 0.5 for s in range(WORD)]
    index_v[...] = sum(jnp.where(seen[s], 1 << s, 0) for s in range(WORD))
    index_copy = pltpu.make_async_copy(index_v, index_s, index_sem)
    index_copy.start()
    gains = [
        jnp.where(seen[s], compact[s * chunks : (s + 1) * chunks, :width], 0.0)
        for s in range(WORD)
    ]

    def part(rows, place):
        return rows[:, place * width : (place + 1) * width]

    def one_step(moved, now):
        return jnp.where(now, part(moved, 0), part(moved, 1))

    def two_steps(moved, now, later):
        return jnp.where(
            later,
            jnp.where(now, part(moved, 5), part(moved, 4)),
            jnp.where(now, part(moved, 3), part(moved, 2)),
        )

    moved = mm(jnp.concatenate(gains[:2], axis=0), moves)
    middle = one_step(moved[:chunks], seen[1]) + gains[1]
    offset = two_steps(moved[:chunks], seen[1], seen[2]) + one_step(moved[chunks:], seen[2])
    offset = offset + gains[2]
    offsets[...] = offset
    index_copy.wait()

    radices = [WORD] + radices_of(chunks)
    levels = []

    def powers_by_steps():
        base = smooth_v[...].T
        for level, radix in enumerate(radices):
            wanted = radix - 1 if level == len(radices) - 1 else radix
            powers = [base]
            while len(powers) < wanted:
                take = min(len(powers), wanted - len(powers))
                more = mm(powers[-1], ready(jnp.concatenate(powers[:take], axis=1)))
                powers += [more[:, i * width : (i + 1) * width] for i in range(take)]
                yield
            if level == 0:
                ends = mm(trans_t, ready(jnp.concatenate(powers, axis=1)))
                yield
                ends = [ends[:, i * width : (i + 1) * width] for i in range(radix)]
                eye_f = (iota((width, width), 0) == iota((width, width), 1)).astype(jnp.float32)
                starts = [l - e for l, e in zip([eye_f] + powers[: radix - 1], ends)]
                levels.append(ready(jnp.concatenate(starts, axis=0)))
                levels.append(ready(jnp.concatenate(ends, axis=1)))
            else:
                levels.append(ready(jnp.concatenate(powers[: radix - 1], axis=0)))
            base = powers[-1]

    side = powers_by_steps()

    eye = iota((width, width), 0) == iota((width, width), 1)
    state = prior_v[:, pl.ds(pl.multiple_of(block * width, width), width)]
    entries[0:1, :] = state
    for c in range(0, chunks, 2):
        terms = words[index_s[c, 0]] * state
        terms = terms + jnp.where(eye, offsets[c : c + 1, :], 0.0)
        column = jnp.sum(terms, axis=1, keepdims=True)
        entries[c + 1 : c + 2, :] = jnp.sum(jnp.where(eye, column, 0.0), axis=0, keepdims=True)
        terms = words_t[index_s[c + 1, 0]] * column
        state = jnp.sum(terms, axis=0, keepdims=True) + offsets[c + 1 : c + 2, :]
        entries[c + 2 : c + 3, :] = state
        next(side, None)
    for _ in side:
        pass

    moved = mm(entries[0:chunks, :], moves)
    filtered = [
        one_step(moved, seen[0]) + gains[0],
        two_steps(moved, seen[0], seen[1]) + middle,
        entries[1 : chunks + 1, :],
    ]
    newest = entries[chunks : chunks + 1, :]

    tail = buf_a.shape[1] - chunks
    for s in range(WORD):
        buf_a[s, chunks:, :] = jnp.zeros((tail, width), jnp.float32)
        buf_b[s, chunks:, :] = jnp.zeros((tail, width), jnp.float32)

    def ahead_of(buf, values, radix, stride):
        for s in range(WORD):
            buf[s, 0:chunks, :] = values[s]
        columns = []
        for i in range(1, radix):
            parts = []
            for s in range(WORD):
                later = s + i * stride
                parts.append(buf[later % WORD, later // WORD : later // WORD + chunks, :])
            columns.append(jnp.concatenate(parts, axis=0))
        return columns

    def by_step(rows):
        return [rows[s * chunks : (s + 1) * chunks] for s in range(WORD)]

    columns = [jnp.concatenate(filtered, axis=0)] + ahead_of(buf_a, filtered, WORD, 1)
    total = mm(jnp.concatenate(columns, axis=1), levels[0])
    finish = mm(jnp.broadcast_to(newest, (16, width)), levels[1])[0:1]
    is_end = iota((chunks, width), 0) == chunks - 1
    total = total + jnp.concatenate(
        [
            jnp.where(is_end, finish[:, i * width : (i + 1) * width], 0.0)
            for i in reversed(range(WORD))
        ],
        axis=0,
    )
    stride = WORD
    for level, radix in enumerate(radices[1:]):
        buf = buf_b if level % 2 == 0 else buf_a
        columns = ahead_of(buf, by_step(total), radix, stride)
        total = total + mm(jnp.concatenate(columns, axis=1), levels[level + 2])
        stride *= radix

    result[...] = choose(gather.T[:, :live], total).reshape(n, cap, width)

    column_of = pl.ds(pl.multiple_of(block * width, width), width)
    for step in range(1, nblocks):
        there = lax.rem(me + step * share, n)
        pltpu.make_async_remote_copy(
            src_ref=result.at[there],
            dst_ref=out_hbm.at[:, column_of],
            send_sem=send_sem2,
            recv_sem=recv_sem2,
            device_id={"tm": there},
            device_id_type=MESH,
        ).start()
    own_out = pltpu.make_async_copy(result.at[me], out_hbm.at[:, column_of], recv_sem2)
    own_out.start()
    sent = got.at[pl.ds(0, n - 1)]
    pltpu.make_async_copy(sent, sent, send_sem).wait()
    sent = result.at[pl.ds(0, nblocks - 1)]
    pltpu.make_async_copy(sent, sent, send_sem2).wait()
    pltpu.make_async_copy(out_hbm, out_hbm, recv_sem2).wait()


def shards(
    observations, outage_mask, group_length, prior_mean, transition, filter_gain, smoother_gain
):
    cap = observations.shape[0]
    nblocks, width, _ = transition.shape
    n = lax.axis_size("tm")
    chunks = n * cap * 3 // 4 // WORD
    reach = max([1] + [(r - 1) * s for r, s in zip(radices_of(chunks), strides_of(chunks))])
    tall = chunks + -(-reach // 8) * 8
    hbm = pl.BlockSpec(memory_space=pltpu.HBM)
    f32 = jnp.float32
    return pl.pallas_call(
        functools.partial(kernel, n),
        out_shape=pltpu.VMEM(observations.shape, f32),
        in_specs=[pl.BlockSpec(memory_space=pltpu.SMEM)] + [hbm] * 6,
        out_specs=pl.BlockSpec(memory_space=pl.ANY),
        scratch_shapes=[
            pltpu.VMEM((cap, nblocks), jnp.int32),
            pltpu.VMEM((1, nblocks * width), f32),
            pltpu.VMEM((cap, nblocks * width), f32),
            pltpu.VMEM((nblocks, 2 * cap, width), f32),
            pltpu.VMEM((n, 2 * cap, width), f32),
            pltpu.VMEM((width, width), f32),
            pltpu.VMEM((width, width), f32),
            pltpu.VMEM((width, width), f32),
            pltpu.VMEM((1 << WORD, width, width), f32),
            pltpu.VMEM((1 << WORD, width, width), f32),
            pltpu.VMEM((chunks, width), jnp.int32),
            pltpu.SMEM((chunks, width), jnp.int32),
            pltpu.VMEM((chunks, width), f32),
            pltpu.VMEM((chunks + 8, width), f32),
            pltpu.VMEM((WORD, tall, width), f32),
            pltpu.VMEM((WORD, tall, width), f32),
            pltpu.VMEM((n, cap, width), f32),
            pltpu.SemaphoreType.DMA((6,)),
            pltpu.SemaphoreType.DMA,
            pltpu.SemaphoreType.DMA,
            pltpu.SemaphoreType.DMA,
            pltpu.SemaphoreType.DMA,
            pltpu.SemaphoreType.DMA,
        ],
        compiler_params=pltpu.CompilerParams(
            collective_id=0, has_side_effects=True, vmem_limit_bytes=48 << 20
        ),
    )(
        group_length,
        *(
            pltpu.with_memory_space_constraint(value, pltpu.HBM)
            for value in (
                outage_mask,
                observations,
                prior_mean.reshape(1, -1),
                transition,
                filter_gain,
                smoother_gain,
            )
        )
    )


def strides_of(chunks):
    strides, span = [], 1
    for radix in radices_of(chunks):
        strides.append(span)
        span *= radix
    return strides


def solution(mesh):
    placed = (
        P(("parts", "tm"), None),
        P(("parts", "tm"), None),
        P(("parts", "tm")),
        P("parts"),
        P(),
        P(),
        P(),
    )
    return jax.shard_map(
        shards, mesh=mesh, in_specs=placed, out_specs=P(("parts", "tm"), None), check_vma=False
    )
```

```python
import functools

import jax
import jax.numpy as jnp
from jax import lax
from jax.experimental import pallas as pl
from jax.experimental.pallas import tpu as pltpu
from jax.sharding import PartitionSpec as P

MESH = pl.DeviceIdType.MESH
WORD = 3
PER = 1


def split(value):
    high = value.astype(jnp.bfloat16)
    return high, (value - high.astype(jnp.float32)).astype(jnp.bfloat16)


def ready(weight):
    high, low = split(weight)
    return jnp.concatenate([high, high, low], axis=0)


def mm(left, right):
    high, low = split(left)
    return jnp.dot(
        jnp.concatenate([high, low, high], axis=1), right, preferred_element_type=jnp.float32
    )


def choose(chosen, values):
    high, low = split(values)
    chosen = chosen.astype(jnp.bfloat16)
    return jnp.dot(
        jnp.concatenate([chosen, chosen], axis=1),
        jnp.concatenate([high, low], axis=0),
        preferred_element_type=jnp.float32,
    )


def radices_of(chunks):
    found, span = [], 1
    for radix in (6, 6, 4, 4, 4, 4):
        if span >= chunks:
            break
        found.append(radix)
        span *= radix
    return found


def iota(shape, axis):
    return lax.broadcasted_iota(jnp.int32, shape, axis)


def kernel(
    n,
    length_ref,
    mask_hbm,
    obs_hbm,
    prior_hbm,
    trans_hbm,
    filt_hbm,
    smooth_hbm,
    out_hbm,
    alive_v,
    got_obs,
    got_mask,
    got_alive,
    prior_v,
    trans_v,
    filt_v,
    smooth_v,
    words,
    words_t,
    index_v,
    index_s,
    offsets,
    entries,
    buf_a,
    buf_b,
    result,
    load_sem,
    send_sem,
    recv_sem,
    out_sem,
    index_sem,
):
    cap, both = got_obs.shape[1:]
    width = trans_v.shape[1]
    nblocks = trans_hbm.shape[0]
    owners = nblocks // PER
    slots = n * cap
    live = slots * 3 // 4
    chunks = live // WORD
    padded = -(-live // width) * width

    me = lax.axis_index("tm")
    is_owner = me < owners
    block = me * PER
    mine = range(PER)

    def own_columns():
        return pl.ds(pl.multiple_of(me * both, both), both)

    loads = [
        pltpu.make_async_copy(source, target, load_sem.at[place])
        for place, (source, target) in enumerate(
            (
                (trans_hbm.at[pl.ds(block, PER)], trans_v),
                (filt_hbm.at[pl.ds(block, PER)], filt_v),
                (smooth_hbm.at[pl.ds(block, PER)], smooth_v),
                (prior_hbm, prior_v),
            )
        )
    ]

    barrier = pltpu.get_barrier_semaphore()

    def greet(there):
        pl.semaphore_signal(barrier, inc=1, device_id={"tm": there}, device_id_type=MESH)

    @pl.when(is_owner)
    def _():
        for load in loads:
            load.start()
        for step in range(1, n):
            greet(lax.rem(me + step, n))

    @pl.when(jnp.logical_not(is_owner))
    def _():
        for owner in range(owners):
            greet(owner)

    length = length_ref[0]
    own_slot = iota((cap, width), 0) * width + iota((cap, width), 1) - me * cap
    alive_v[...] = ((own_slot >= 0) & (own_slot < length)).astype(jnp.float32)

    @pl.when(is_owner)
    def _():
        pl.semaphore_wait(barrier, n - 1)

    @pl.when(jnp.logical_not(is_owner))
    def _():
        pl.semaphore_wait(barrier, owners)

    for owner in range(owners):
        parcels = (
            (alive_v, got_alive.at[me]),
            (mask_hbm, got_mask.at[me]),
            (obs_hbm.at[:, owner * both : (owner + 1) * both], got_obs.at[me]),
        )

        @pl.when(me != owner)
        def _():
            for kind, (source, target) in enumerate(parcels):
                pltpu.make_async_remote_copy(
                    src_ref=source,
                    dst_ref=target,
                    send_sem=send_sem.at[kind],
                    recv_sem=recv_sem.at[kind],
                    device_id={"tm": owner},
                    device_id_type=MESH,
                ).start()

        @pl.when(me == owner)
        def _():
            for kind, (source, target) in enumerate(parcels):
                pltpu.make_async_copy(source, target, recv_sem.at[kind]).start()

    @pl.when(is_owner)
    def _():
        for load in loads:
            load.wait()
        trans = [trans_v[j] for j in mine]
        gain = [filt_v[j] for j in mine]
        trans_t = [trans[j].T for j in mine]
        update = [trans[j] - mm(gain[j], ready(trans[j])) for j in mine]
        update_t = [update[j].T for j in mine]
        gain_t = [ready(gain[j].T) for j in mine]
        step_t = [ready(jnp.concatenate([update_t[j], trans_t[j]], axis=1)) for j in mine]

        def tile(whole, row, column):
            return whole[row * width : (row + 1) * width, column * width : (column + 1) * width]

        for j in mine:
            rows = jnp.concatenate([trans[j], update[j]], axis=0)
            square = mm(rows, ready(jnp.concatenate([trans[j], update[j]], axis=1)))
            square_t = mm(jnp.concatenate([trans_t[j], update_t[j]], axis=0), step_t[j])
            pairs = [tile(square, hi, lo) for hi in range(2) for lo in range(2)]
            pairs_t = [tile(square_t, lo, 1 - hi) for hi in range(2) for lo in range(2)]
            cube = mm(rows, ready(jnp.concatenate(pairs, axis=1)))
            cube_t = mm(jnp.concatenate(pairs_t, axis=0), step_t[j])
            for last in range(2):
                for p in range(4):
                    words[8 * j + 4 * last + p] = tile(cube, last, p)
                    words_t[8 * j + 4 * last + p] = tile(cube_t, p, 1 - last)

        for kind, got in enumerate((got_alive, got_mask, got_obs)):
            pltpu.make_async_copy(got, got, recv_sem.at[kind]).wait()
        readings = got_obs[...].reshape(slots, both)
        gained_slot = [
            mm(readings[:, j * width : (j + 1) * width], gain_t[j]) for j in mine
        ]
        alive_sum = jnp.sum(got_alive[...], axis=0)
        alive_row = jnp.concatenate(
            [alive_sum[k : k + 1] for k in range(slots // width)], axis=1
        )
        earlier = (iota((slots, slots), 0) < iota((slots, slots), 1)).astype(jnp.bfloat16)
        place = jnp.dot(
            jnp.broadcast_to(alive_row, (16, slots)).astype(jnp.bfloat16),
            earlier,
            preferred_element_type=jnp.float32,
        )[0:1]
        place = jnp.where(alive_row > 0.5, place, -1.0)
        mask = got_mask[...].reshape(slots, nblocks).astype(jnp.float32).astype(jnp.bfloat16)
        which = jnp.concatenate(
            [(iota((nblocks, width), 0) == block + j).astype(jnp.bfloat16) for j in mine], axis=1
        )
        seen_slot = jnp.dot(mask, which, preferred_element_type=jnp.float32)
        row = iota((padded, slots), 0)
        within = sum((row >= s * chunks).astype(jnp.int32) for s in range(1, WORD))
        step_of = WORD * (row - within * chunks) + within
        step_of = jnp.where(row < live, step_of, -2).astype(jnp.float32)
        gather = (jnp.broadcast_to(place, (padded, slots)) == step_of).astype(jnp.float32)
        seen_rows = jnp.dot(
            gather.astype(jnp.bfloat16),
            seen_slot.astype(jnp.bfloat16),
            preferred_element_type=jnp.float32,
        )

        def by_step(rows):
            return [rows[s * chunks : (s + 1) * chunks] for s in range(WORD)]

        seen = [
            [part > 0.5 for part in by_step(seen_rows[:, j * width : (j + 1) * width])]
            for j in mine
        ]
        for j in mine:
            index_v[j] = sum(jnp.where(seen[j][s], 1 << s, 0) for s in range(WORD))
        index_copy = pltpu.make_async_copy(index_v, index_s, index_sem)
        index_copy.start()
        gain_rows = choose(gather, jnp.concatenate(gained_slot, axis=1))
        gains = [
            [
                jnp.where(seen[j][s], part, 0.0)
                for s, part in enumerate(by_step(gain_rows[:, j * width : (j + 1) * width]))
            ]
            for j in mine
        ]

        def advance(j, state, s):
            moved = mm(state, step_t[j])
            return jnp.where(seen[j][s], moved[:, :width], moved[:, width:]) + gains[j][s]

        offset = [gains[j][0] for j in mine]
        for s in range(1, WORD):
            offset = [advance(j, offset[j], s) for j in mine]
        for j in mine:
            offsets[j] = offset[j]
        index_copy.wait()

        radices = [WORD] + radices_of(chunks)

        def powers_by_steps(j, levels):
            base = smooth_v[j].T
            for level, radix in enumerate(radices):
                wanted = radix - 1 if level == len(radices) - 1 else radix
                powers = [base]
                while len(powers) < wanted:
                    take = min(len(powers), wanted - len(powers))
                    more = mm(powers[-1], ready(jnp.concatenate(powers[:take], axis=1)))
                    powers += [more[:, i * width : (i + 1) * width] for i in range(take)]
                    yield
                if level == 0:
                    ends = mm(trans_t[j], ready(jnp.concatenate(powers, axis=1)))
                    yield
                    ends = [ends[:, i * width : (i + 1) * width] for i in range(radix)]
                    eye_f = (iota((width, width), 0) == iota((width, width), 1)).astype(
                        jnp.float32
                    )
                    starts = [l - e for l, e in zip([eye_f] + powers[: radix - 1], ends)]
                    levels.append(ready(jnp.concatenate(starts, axis=0)))
                    levels.append(ready(jnp.concatenate(ends, axis=1)))
                else:
                    levels.append(ready(jnp.concatenate(powers[: radix - 1], axis=0)))
                base = powers[-1]

        levels = [[] for j in mine]
        side = [powers_by_steps(j, levels[j]) for j in mine]

        eye = iota((width, width), 0) == iota((width, width), 1)
        state = [
            prior_v[:, pl.ds(pl.multiple_of((block + j) * width, width), width)] for j in mine
        ]
        for j in mine:
            entries[j, 0:1, :] = state[j]
        for c in range(0, chunks, 2):
            column = [None] * PER
            for j in mine:
                terms = words[8 * j + index_s[j, c, 0]] * state[j]
                terms = terms + jnp.where(eye, offsets[j, c : c + 1, :], 0.0)
                column[j] = jnp.sum(terms, axis=1, keepdims=True)
            for j in mine:
                entries[j, c + 1 : c + 2, :] = jnp.sum(
                    jnp.where(eye, column[j], 0.0), axis=0, keepdims=True
                )
                terms = words_t[8 * j + index_s[j, c + 1, 0]] * column[j]
                state[j] = jnp.sum(terms, axis=0, keepdims=True) + offsets[j, c + 1 : c + 2, :]
                entries[j, c + 2 : c + 3, :] = state[j]
                next(side[j], None)
        for j in mine:
            for _ in side[j]:
                pass

        state = [entries[j, 0:chunks, :] for j in mine]
        filtered = [[] for j in mine]
        for s in range(WORD - 1):
            for j in mine:
                state[j] = advance(j, state[j], s)
                filtered[j].append(state[j])
        for j in mine:
            filtered[j].append(entries[j, 1 : chunks + 1, :])

        tail = buf_a.shape[2] - chunks
        for j in mine:
            for s in range(WORD):
                buf_a[j, s, chunks:, :] = jnp.zeros((tail, width), jnp.float32)
                buf_b[j, s, chunks:, :] = jnp.zeros((tail, width), jnp.float32)

        def ahead_of(buf, j, values, radix, stride):
            for s in range(WORD):
                buf[j, s, 0:chunks, :] = values[s]
            columns = []
            for i in range(1, radix):
                parts = []
                for s in range(WORD):
                    later = s + i * stride
                    first = later // WORD
                    parts.append(buf[j, later % WORD, first : first + chunks, :])
                columns.append(jnp.concatenate(parts, axis=0))
            return columns

        total = [None] * PER
        for j in mine:
            columns = [jnp.concatenate(filtered[j], axis=0)]
            columns += ahead_of(buf_a, j, filtered[j], WORD, 1)
            total[j] = mm(jnp.concatenate(columns, axis=1), levels[j][0])
            newest = jnp.broadcast_to(entries[j, chunks : chunks + 1, :], (16, width))
            finish = mm(newest, levels[j][1])[0:1]
            is_end = iota((chunks, width), 0) == chunks - 1
            total[j] = total[j] + jnp.concatenate(
                [
                    jnp.where(is_end, finish[:, i * width : (i + 1) * width], 0.0)
                    for i in reversed(range(WORD))
                ],
                axis=0,
            )
        stride = WORD
        for level, radix in enumerate(radices[1:]):
            buf = buf_b if level % 2 == 0 else buf_a
            for j in mine:
                columns = ahead_of(buf, j, by_step(total[j]), radix, stride)
                total[j] = total[j] + mm(
                    jnp.concatenate(columns, axis=1), levels[j][level + 2]
                )
            stride *= radix

        spread = gather.T[:, :live]
        result[...] = choose(spread, jnp.concatenate(total, axis=1)).reshape(n, cap, both)

        for there in range(n):

            @pl.when(me != there)
            def _():
                pltpu.make_async_remote_copy(
                    src_ref=result.at[there],
                    dst_ref=out_hbm.at[:, own_columns()],
                    send_sem=send_sem.at[3],
                    recv_sem=out_sem,
                    device_id={"tm": there},
                    device_id_type=MESH,
                ).start()

            @pl.when(me == there)
            def _():
                pltpu.make_async_copy(
                    result.at[there], out_hbm.at[:, own_columns()], out_sem
                ).start()

        for kind, got in enumerate((got_alive, got_mask, got_obs)):
            sent = got.at[pl.ds(0, owners - 1)]
            pltpu.make_async_copy(sent, sent, send_sem.at[kind]).wait()
        sent = result.at[pl.ds(0, n - 1)]
        pltpu.make_async_copy(sent, sent, send_sem.at[3]).wait()

    @pl.when(jnp.logical_not(is_owner))
    def _():
        for kind, got in enumerate((got_alive, got_mask, got_obs)):
            sent = got.at[pl.ds(0, owners)]
            pltpu.make_async_copy(sent, sent, send_sem.at[kind]).wait()

    pltpu.make_async_copy(out_hbm, out_hbm, out_sem).wait()


def shards(
    observations, outage_mask, group_length, prior_mean, transition, filter_gain, smoother_gain
):
    cap = observations.shape[0]
    nblocks, width, _ = transition.shape
    n = lax.axis_size("tm")
    chunks = n * cap * 3 // 4 // WORD
    reach = max([1] + [(r - 1) * s for r, s in zip(radices_of(chunks), strides_of(chunks))])
    tall = chunks + -(-reach // 8) * 8
    hbm = pl.BlockSpec(memory_space=pltpu.HBM)
    f32 = jnp.float32
    return pl.pallas_call(
        functools.partial(kernel, n),
        out_shape=pltpu.VMEM(observations.shape, f32),
        in_specs=[pl.BlockSpec(memory_space=pltpu.SMEM)] + [hbm] * 6,
        out_specs=pl.BlockSpec(memory_space=pl.ANY),
        scratch_shapes=[
            pltpu.VMEM((cap, width), f32),
            pltpu.VMEM((n, cap, PER * width), f32),
            pltpu.VMEM((n, cap, nblocks), jnp.int32),
            pltpu.VMEM((n, cap, width), f32),
            pltpu.VMEM((1, nblocks * width), f32),
            pltpu.VMEM((PER, width, width), f32),
            pltpu.VMEM((PER, width, width), f32),
            pltpu.VMEM((PER, width, width), f32),
            pltpu.VMEM((PER << WORD, width, width), f32),
            pltpu.VMEM((PER << WORD, width, width), f32),
            pltpu.VMEM((PER, chunks, width), jnp.int32),
            pltpu.SMEM((PER, chunks, width), jnp.int32),
            pltpu.VMEM((PER, chunks, width), f32),
            pltpu.VMEM((PER, chunks + 8, width), f32),
            pltpu.VMEM((PER, WORD, tall, width), f32),
            pltpu.VMEM((PER, WORD, tall, width), f32),
            pltpu.VMEM((n, cap, PER * width), f32),
            pltpu.SemaphoreType.DMA((4,)),
            pltpu.SemaphoreType.DMA((4,)),
            pltpu.SemaphoreType.DMA((3,)),
            pltpu.SemaphoreType.DMA,
            pltpu.SemaphoreType.DMA,
        ],
        compiler_params=pltpu.CompilerParams(
            collective_id=0, has_side_effects=True, vmem_limit_bytes=48 << 20
        ),
    )(
        group_length,
        *(
            pltpu.with_memory_space_constraint(value, pltpu.HBM)
            for value in (
                outage_mask,
                observations,
                prior_mean.reshape(1, -1),
                transition,
                filter_gain,
                smoother_gain,
            )
        )
    )


def strides_of(chunks):
    strides, span = [], 1
    for radix in radices_of(chunks):
        strides.append(span)
        span *= radix
    return strides


def solution(mesh):
    placed = (
        P(("parts", "tm"), None),
        P(("parts", "tm"), None),
        P(("parts", "tm")),
        P("parts"),
        P(),
        P(),
        P(),
    )
    return jax.shard_map(
        shards, mesh=mesh, in_specs=placed, out_specs=P(("parts", "tm"), None), check_vma=False
    )
```
